128 devices in a mesh: lon: 16 (over y, z_lo, core), lat: 8 (over z_hi, x).
Axes of the slice: x: 4, y: 4, z: 4 (z_hi: 2, z_lo: 2; z = z_hi * 2 + z_lo), core: 2. Of those that a mesh axis runs over, the one named last changes fastest.
Arguments:
- inputs: bfloat16 [128, 1440, 384], P('lat', 'lon'), may hold values from -6 to 6
- basis: bfloat16 [128, 8, 5, 91], replicated, may hold values from -0.59765625 to 0.59765625
- spans: int32 [128], replicated, may hold values from 1 to 45, as said below
- weight: bfloat16 [3072, 384], replicated, may hold values from -0.109375 to 0.109375
- cotangent: bfloat16 [128, 1440, 384], P('lat', 'lon'), may hold values from -6 to 6
Outputs:
- output: bfloat16 [128, 1440, 384], P('lat', 'lon')
- grad_inputs: bfloat16 [128, 1440, 384], P('lat', 'lon')
- grad_weight: float32 [3072, 384], P(('lon', 'lat'))
The draws below stay inside these ranges and needn't reach their ends.
Inputs may be any that keep to these rules, and one draw needn't show every extreme that they name: `spans`: the first row's half-width is 45.
All inputs are finite; a program needn't handle non-finite values.
Results may differ from the reference program's by a relative error of at most 0.0065.
Values may be sent and summed in bfloat16 or wider, within the bound.
A program may use at most 448 MiB of HBM per device.

```python
import math
import jax
import jax.numpy as jnp
from jax import lax

C = 384
CO = 384
K = 8
RR = 2
SMAX = 45
NLON = 1440
NLAT = 128


def draw_spans(key, part):
    key = jax.random.fold_in(key, 11)
    row_index = jnp.arange(NLAT, dtype=jnp.int32)
    base_span = SMAX * 4 // (row_index + 4)
    drawn_span = jax.random.randint(key, (NLAT,), 1, SMAX + 1, dtype=jnp.int32)
    spread_rows = jnp.clip(jnp.maximum(base_span, drawn_span), 1, SMAX)
    return jnp.where(row_index == 0, SMAX, spread_rows).astype(jnp.int32)


def block_scale(rng, dims, cuts, low, largest):
    def one(position, shards_of):
        draws = jax.random.uniform(jax.random.fold_in(jax.random.fold_in(rng, 6), position), (shards_of,), jnp.float32, low / len(cuts), largest / len(cuts))
        return jnp.repeat(jnp.exp(draws), dims[position] // shards_of).reshape((-1,) + (1,) * (len(dims) - position - 1))

    level = one(*cuts[0])
    for cut in cuts[1:]:
        level = level * one(*cut)
    return level


def normal_values(own_key, extent, scale, reach, pieces=(), held_as=jnp.bfloat16):
    level = block_scale(own_key, extent, pieces, -0.22, 0.18) if pieces else 1.0
    drawn = jax.random.normal(own_key, extent, jnp.float32) * scale * level
    return jnp.minimum(jnp.maximum(drawn, -reach), reach).astype(held_as)


def setup_inputs(seed: int = 0) -> dict:
    key_of = jax.random.split(jax.random.key(seed), 6)
    inputs = normal_values(key_of[0], (NLAT, NLON, C), 1.0, 6.0, ((0, 8), (1, 16)))
    basis = normal_values(key_of[1], (NLAT, K, 2 * RR + 1, 2 * SMAX + 1), 0.1, 0.59765625)
    spans = draw_spans(jax.random.fold_in(key_of[5], 71), 0)
    weight = normal_values(key_of[3], (K * C, CO), (K * C) ** -0.5, 0.109375)
    cotangent = normal_values(key_of[4], (NLAT, NLON, CO), 1.0, 6.0, ((0, 8), (1, 16)))
    return {"inputs": inputs, "basis": basis, "spans": spans, "weight": weight, "cotangent": cotangent}


def reference(inputs, basis, spans, weight, cotangent):
    lat_total, lon_total, channels = inputs.shape
    tap_count = 2 * SMAX + 1
    reach_rows = 2 * RR + 1
    offsets = jnp.abs(jnp.arange(tap_count, dtype=jnp.int32) - SMAX)
    keep_mask = (offsets[None, :] <= spans[:, None]).astype(jnp.float32)
    kernel = basis.astype(jnp.float32) * keep_mask[:, None, None, :]
    fill_cols = ((0, 0), (0, 0), (0, 0), (0, lon_total - tap_count))
    forward_taps = jnp.roll(jnp.pad(kernel[..., ::-1], fill_cols), -SMAX, axis=3)
    backward_taps = jnp.roll(jnp.pad(kernel, fill_cols), -SMAX, axis=3)
    forward_hat = jnp.fft.rfft(forward_taps, axis=3)
    backward_hat = jnp.fft.rfft(backward_taps, axis=3)
    padded_in = jnp.pad(inputs.astype(jnp.float32), ((RR, RR), (0, 0), (0, 0)))
    input_hat = jnp.fft.rfft(padded_in, axis=1)

    def row_step(state_pair, row_index):
        grad_hat, grad_total = state_pair
        near_rows = lax.dynamic_slice_in_dim(input_hat, row_index, reach_rows, 0)
        mixed_hat = jnp.einsum('kaf,afc->fkc', forward_hat[row_index], near_rows)
        mixed_row = jnp.fft.irfft(mixed_hat, n=lon_total, axis=0).reshape(lon_total, K * channels).astype(jnp.bfloat16)
        output_row = jnp.dot(mixed_row, weight, preferred_element_type=jnp.float32).astype(jnp.bfloat16)
        cotangent_row = cotangent[row_index]
        grad_row = lax.dot_general(cotangent_row, weight, (((1,), (1,)), ((), ())), preferred_element_type=jnp.float32).astype(jnp.bfloat16)
        grad_total = grad_total + lax.dot_general(mixed_row, cotangent_row, (((0,), (0,)), ((), ())), preferred_element_type=jnp.float32)
        grad_row_hat = jnp.fft.rfft(grad_row.astype(jnp.float32).reshape(lon_total, K, channels), axis=0)
        partial_value = jnp.einsum('kaf,fkc->afc', backward_hat[row_index], grad_row_hat)
        current = lax.dynamic_slice_in_dim(grad_hat, row_index, reach_rows, 0)
        grad_hat = lax.dynamic_update_slice_in_dim(grad_hat, current + partial_value, row_index, 0)
        return ((grad_hat, grad_total), output_row)
    start_pair = (jnp.zeros_like(input_hat), jnp.zeros((K * channels, weight.shape[1]), jnp.float32))
    final_pair, output = lax.scan(row_step, start_pair, jnp.arange(lat_total, dtype=jnp.int32))
    grad_hat, grad_total = final_pair
    grad_field = jnp.fft.irfft(grad_hat, n=lon_total, axis=1)[RR:RR + lat_total]
    grad_inputs = grad_field.astype(jnp.bfloat16)
    grad_weight = grad_total * (1.0 / math.sqrt(lat_total * lon_total))
    return (output, grad_inputs, grad_weight)
```

```python
import functools
import math

import jax
import jax.numpy as jnp
from jax import lax
from jax.experimental import pallas as pl
from jax.experimental.pallas import tpu as pltpu
from jax.sharding import PartitionSpec as P

RR = 2
SMAX = 45
REACH = 2 * RR + 1
TAPS = 2 * SMAX + 1
B = 48
W = 144
LEAD = 3
BAND = 768
MESH = pl.DeviceIdType.MESH
F32 = jnp.float32
BF16 = jnp.bfloat16


def dot(a, b):
    return jnp.dot(a, b, preferred_element_type=F32)


def kernel(
    cot_hbm, x_hbm, taps_hbm, weight_hbm,
    out_ref, gin_ref, gw_ref,
    wc, wx, own_c, own_x, sl_c, sl_x, rst_c, rst_x,
    bands, feat, weight, weight_t, xt, taps, rtaps,
    tmp, gown, cs, cr, xs, xr, s2, ys, yr, s3, zr,
    load_sem, hs_send, hs_recv, cs_send, cs_recv, xs_send, xs_recv,
    ys_send, ys_recv, zs_send, zs_recv,
):
    rows, cols, C = x_hbm.shape
    K = weight_hbm.shape[0] // C
    lon, lat = lax.axis_index("lon"), lax.axis_index("lat")
    nlon, nlat = lax.axis_size("lon"), lax.axis_size("lat")
    core, zl, y = lon % 2, (lon // 2) % 2, lon // 4
    x, zh = lat % 4, lat // 4
    right, left = lax.rem(lon + 1, nlon), lax.rem(lon + nlon - 1, nlon)
    not_first, not_last = lat > 0, lat < nlat - 1

    def at(lon_, lat_):
        return {"lon": lon_, "lat": lat_}

    def lon_of(y_, zl_, core_):
        return (y_ * 2 + zl_) * 2 + core_

    core_dev = at(lon_of(y, zl, 1 - core), lat)
    x_devs = [at(lon, zh * 4 + (x + d) % 4) for d in (1, 2, 3)]
    y_devs = [at(lon_of((y + d) % 4, zl, core), lat) for d in (1, 2, 3)]
    z_steps = ((0, 1), (1, 0), (1, 1))
    z_devs = [
        at(lon_of(y, (zl + a) % 2, core), ((zh + b) % 2) * 4 + x) for a, b in z_steps
    ]

    loads = [
        pltpu.make_async_copy(cot_hbm, gin_ref, load_sem.at[0]),
        pltpu.make_async_copy(x_hbm, out_ref, load_sem.at[1]),
        pltpu.make_async_copy(taps_hbm, taps, load_sem.at[2]),
        pltpu.make_async_copy(weight_hbm, weight, load_sem.at[3]),
    ]
    for load in loads:
        load.start()

    barrier = pltpu.get_barrier_semaphore()

    def greet(device):
        pl.semaphore_signal(barrier, inc=1, device_id=device, device_id_type=MESH)

    for device in [at(left, lat), at(right, lat), core_dev] + x_devs + y_devs + z_devs:
        greet(device)

    @pl.when(not_first)
    def _():
        for lon_ in (left, lon, right):
            greet(at(lon_, lat - 1))

    @pl.when(not_last)
    def _():
        for lon_ in (left, lon, right):
            greet(at(lon_, lat + 1))

    chunks = ((0, 8), (8, 4), (12, 4))

    def halo(t, own, sl, w, rst):
        plan = []
        for start, n in chunks:
            plan.append((sl.at[pl.ds(start, n)],
                         w.at[pl.ds(RR + start, n), pl.ds(0, B), pl.ds(0, C)],
                         at(right, lat), None, None))
        for start, n in chunks:
            plan.append((own.at[pl.ds(start, n), pl.ds(0, B)],
                         rst.at[pl.ds(RR + start, n)], at(left, lat), None, None))
        low, high = pl.ds(0, RR), pl.ds(rows - RR, RR)
        for src, dst, step, here, there in (
            (high, pl.ds(0, RR), 1, not_last, not_first),
            (low, pl.ds(rows + RR, RR), -1, not_first, not_last),
        ):
            plan.append((own.at[src], w.at[dst, pl.ds(0, 2 * B), pl.ds(C, C)],
                         at(lon, lat + step), here, there))
            plan.append((sl.at[src], w.at[dst, pl.ds(0, B), pl.ds(0, C)],
                         at(right, lat + step), here, there))
            plan.append((own.at[src, pl.ds(0, B)], rst.at[dst],
                         at(left, lat + step), here, there))
        return [
            (pltpu.make_async_remote_copy(
                src_ref=src, dst_ref=dst, send_sem=hs_send.at[t, i],
                recv_sem=hs_recv.at[t, i], device_id=device, device_id_type=MESH),
             here, there)
            for i, (src, dst, device, here, there) in enumerate(plan)
        ]

    halo_c = halo(0, own_c, sl_c, wc, rst_c)
    halo_x = halo(1, own_x, sl_x, wx, rst_x)

    def guarded(condition, action):
        if condition is None:
            action()
        else:
            pl.when(condition)(action)

    def start(plan, indices):
        for i in indices:
            guarded(plan[i][1], plan[i][0].start)

    def arrive(plan, indices):
        for i in indices:
            guarded(plan[i][2], plan[i][0].wait_recv)

    order = (0, 3, 6, 7, 8, 9, 10, 11, 1, 4, 2, 5)

    def stage(raw, own, sl):
        def step(p, _):
            own[p, 0:cols] = raw[p]
            own[p, cols:2 * B] = jnp.zeros((2 * B - cols, C), BF16)
            sl[p] = raw[p, cols - B:cols]
            return 0
        lax.fori_loop(0, rows, step, 0)

    def place(own, w):
        def step(p, _):
            w[p + RR, B:B + cols, 0:C] = own[p, 0:cols]
            w[p + RR, 0:2 * B, C:2 * C] = own[p]
            return 0
        lax.fori_loop(0, rows, step, 0)

        def pad(p, _):
            w[p, B + cols:W, C:2 * C] = jnp.zeros((W - B - cols, C), BF16)
            return 0
        lax.fori_loop(0, rows + 2 * RR, pad, 0)

        def clear(first):
            for p in range(RR):
                w[first + p] = jnp.zeros((W, 2 * C), BF16)

        pl.when(lat == 0)(lambda: clear(0))
        pl.when(lat == nlat - 1)(lambda: clear(rows + RR))

    def right_edge(first, n, w, rst):
        def step(j, _):
            p = first + j
            r = rst[p]
            w[p, cols:cols + B, C:2 * C] = r
            w[p, B + cols:W, 0:C] = r[0:W - B - cols]
            return 0
        lax.fori_loop(0, n, step, 0)

    def outer_rows(first, w, rst):
        for p in range(RR):
            w[first + p, B:B + cols, 0:C] = w[first + p, 0:cols, C:2 * C]
        right_edge(first, RR, w, rst)

    def build_band(row_taps, i):
        for k in range(K):
            v = jnp.broadcast_to(row_taps[k:k + 1], (B, BAND))
            v = pltpu.roll(v, 0, 1, stride=1, stride_axis=0)
            bands[i, k * B:(k + 1) * B] = v.astype(BF16)

    def convolve(plan, w, rst, between):
        def group(g, _):
            for n, (first, count) in enumerate(chunks):
                @pl.when(g == n)
                def _():
                    arrive(plan, (n, 3 + n))
                    right_edge(RR + first, count, w, rst)
                    between(n)

            @pl.when(g == len(chunks))
            def _():
                arrive(plan, (6, 7, 8, 9, 10, 11))
                pl.when(not_first)(lambda: outer_rows(0, w, rst))
                pl.when(not_last)(lambda: outer_rows(rows + RR, w, rst))

            for u in range(4):
                outer = u if u < RR else rows - 4 + u
                i = jnp.where(g < len(chunks), RR + 4 * g + u, outer)
                window = w[pl.ds(i, REACH)].reshape(REACH * W, 2 * C)
                acc = dot(bands[i, :, 0:REACH * W], window).astype(BF16)
                for k in range(K):
                    for b in range(2):
                        place_at = pl.ds(pl.multiple_of(i * 2 * B + b * B, 16), B)
                        feat[place_at, k * C:(k + 1) * C] = (
                            acc[k * B:(k + 1) * B, b * C:(b + 1) * C])
            return 0
        lax.fori_loop(0, len(chunks) + 1, group, 0)

    loads[0].wait()
    stage(gin_ref, own_c, sl_c)
    pl.semaphore_wait(
        barrier, 12 + jnp.where(not_first, 3, 0) + jnp.where(not_last, 3, 0))
    start(halo_c, order)
    place(own_c, wc)

    loads[1].wait()
    stage(out_ref, own_x, sl_x)
    place(own_x, wx)
    for g in range(4):
        xt[:, g * C:(g + 1) * C] = own_x[4 * g:4 * g + 4].reshape(C, C).T

    loads[2].wait()
    flip = (lax.broadcasted_iota(jnp.int32, (BAND, BAND), 0)
            + lax.broadcasted_iota(jnp.int32, (BAND, BAND), 1))
    flip = jnp.where(flip == (REACH - 1) * W + 2 * B, 1.0, 0.0).astype(BF16)
    rtaps[...] = dot(
        taps[...].reshape((rows + 2 * RR) * K, BAND).astype(BF16), flip
    ).reshape(rows + 2 * RR, K, BAND)
    lane = lax.broadcasted_iota(jnp.int32, (K, BAND), 1)

    def reverse_band(i, _):
        v = rtaps[i]
        for a in range(1, REACH):
            v = jnp.where(lane >= a * W, rtaps[i + a], v)
        build_band(v, i)
        return 0
    lax.fori_loop(0, rows, reverse_band, 0)

    loads[3].wait()

    def turn(k, _):
        at_k = pl.ds(pl.multiple_of(k * C, C), C)
        weight_t[at_k] = weight[at_k].T
        return 0
    lax.fori_loop(0, K, turn, 0)

    def send_x(n):
        if n == 1:
            start(halo_x, order)

    convolve(halo_c, wc, rst_c, send_x)

    def core_copy(j):
        two = pl.ds(2 * j, 2)
        return pltpu.make_async_remote_copy(
            src_ref=cs.at[two], dst_ref=cr.at[two], send_sem=cs_send.at[j],
            recv_sem=cs_recv.at[j], device_id=core_dev, device_id_type=MESH)

    def x_copy(d, j):
        two = pl.ds(2 * j, 2)
        return pltpu.make_async_remote_copy(
            src_ref=xs.at[d, two], dst_ref=xr.at[d, two], send_sem=xs_send.at[d, j],
            recv_sem=xs_recv.at[d, j], device_id=x_devs[d], device_id_type=MESH)

    def quarter(k, x_):
        return jnp.concatenate(
            [gown[k, pl.ds(pl.multiple_of(x_ * 24, 8), 24)],
             gown[k, pl.ds(pl.multiple_of(96 + x_ * 24, 8), 24)]], axis=0)

    def x_stage(j):
        core_copy(j).wait_recv()
        for h in range(2):
            k = 2 * j + h
            gown[k] = gown[k] + cr[k].astype(F32)
            for d in range(3):
                xs[d, k] = quarter(k, (x + d + 1) % 4).astype(BF16)
        for d in range(3):
            x_copy(d, j).start()

    half = C // 2

    def grad_pair(j, _):
        acc = dot(xt[...], feat[:, pl.ds(pl.multiple_of(j * 2 * C, 2 * C), 2 * C)])
        for u in range(4):
            build_band(taps[RR + 4 * j + u], 4 * j + u)
        for h in range(2):
            tmp[h] = acc[:, h * C:(h + 1) * C]
        for h in range(2):
            k = 2 * j + h
            gown[k] = tmp[h, pl.ds(pl.multiple_of(core * half, half), half)]
            cs[k] = tmp[h, pl.ds(pl.multiple_of((1 - core) * half, half), half)].astype(BF16)
        core_copy(j).start()
        pl.when(j > 0)(lambda: x_stage(j - 1))
        return 0
    lax.fori_loop(0, K // 2, grad_pair, 0)
    x_stage(K // 2 - 1)

    def mix(matrix, result):
        per = rows // 2

        def step(j, _):
            m = per * 2 * B
            acc = dot(feat[pl.ds(pl.multiple_of(j * m, 16), m)], matrix[...]).astype(BF16)
            for i in range(per):
                result[j * per + i] = acc[i * 2 * B:i * 2 * B + cols]
            return 0
        lax.fori_loop(0, 2, step, 0)

    mix(weight_t, gin_ref)
    convolve(halo_x, wx, rst_x, lambda n: None)

    def y_copy(d):
        return pltpu.make_async_remote_copy(
            src_ref=ys.at[d], dst_ref=yr.at[d], send_sem=ys_send.at[d],
            recv_sem=ys_recv.at[d], device_id=y_devs[d], device_id_type=MESH)

    for j in range(K // 2):
        for d in range(3):
            x_copy(d, j).wait_recv()

    def add_x(k, _):
        s2[k] = quarter(k, x) + sum(xr[d, k].astype(F32) for d in range(3))
        return 0
    lax.fori_loop(0, K, add_x, 0)
    for d in range(3):
        ys[d] = s2[pl.ds(((y + d + 1) % 4) * 2, 2)].astype(BF16)
        y_copy(d).start()

    mix(weight, out_ref)

    def z_copy(d):
        a, b = z_steps[d]
        src = s3.at[(zl + a) % 2, pl.ds(pl.multiple_of(((zh + b) % 2) * 24, 8), 24)]
        return pltpu.make_async_remote_copy(
            src_ref=src, dst_ref=zr.at[d], send_sem=zs_send.at[d],
            recv_sem=zs_recv.at[d], device_id=z_devs[d], device_id_type=MESH)

    for d in range(3):
        y_copy(d).wait_recv()
    s3[...] = s2[pl.ds(y * 2, 2)] + sum(yr[d].astype(F32) for d in range(3))
    for d in range(3):
        z_copy(d).start()
    for d in range(3):
        z_copy(d).wait_recv()
    total = s3[zl, pl.ds(pl.multiple_of(zh * 24, 8), 24)] + sum(zr[d] for d in range(3))
    scale = 1.0 / math.sqrt(rows * nlat * cols * nlon)
    gw_ref[...] = total * scale

    for plan in (halo_c, halo_x):
        for copy, here, _ in plan:
            guarded(here, copy.wait_send)
    for j in range(K // 2):
        core_copy(j).wait_send()
        for d in range(3):
            x_copy(d, j).wait_send()
    for d in range(3):
        y_copy(d).wait_send()
        z_copy(d).wait_send()


def shards(inputs, basis, spans, weight, cotangent):
    rows, cols, C = inputs.shape
    K = weight.shape[0] // C
    ext = rows + 2 * RR
    first_row = lax.axis_index("lat") * rows
    offsets = jnp.abs(jnp.arange(TAPS, dtype=jnp.int32) - SMAX)
    padded = jnp.pad(basis, ((RR, RR), (0, 0), (0, 0), (0, 0)))
    own_basis = lax.dynamic_slice_in_dim(padded, first_row, ext, 0).astype(F32)
    own_spans = lax.dynamic_slice_in_dim(jnp.pad(spans, (RR, RR)), first_row, ext, 0)
    keep = (offsets[None, :] <= own_spans[:, None])[:, None, None, :]
    masked = jnp.where(keep, own_basis, 0.0)
    taps = sum(
        jnp.pad(masked[:, :, a],
                ((0, 0), (0, 0), (a * W + LEAD, BAND - a * W - LEAD - TAPS)))
        for a in range(REACH)
    )
    vmem = pl.BlockSpec(memory_space=pltpu.VMEM)
    anywhere = pl.BlockSpec(memory_space=pl.ANY)
    own_cols = 2 * B
    dma = pltpu.SemaphoreType.DMA
    half = C // 2
    scratch = [
        pltpu.VMEM((ext, W, 2 * C), BF16),
        pltpu.VMEM((ext, W, 2 * C), BF16),
        pltpu.VMEM((rows, own_cols, C), BF16),
        pltpu.VMEM((rows, own_cols, C), BF16),
        pltpu.VMEM((rows, B, C), BF16),
        pltpu.VMEM((rows, B, C), BF16),
        pltpu.VMEM((ext, B, C), BF16),
        pltpu.VMEM((ext, B, C), BF16),
        pltpu.VMEM((rows, K * B, BAND), BF16),
        pltpu.VMEM((rows * own_cols, K * C), BF16),
        pltpu.VMEM((K * C, C), BF16),
        pltpu.VMEM((K * C, C), BF16),
        pltpu.VMEM((C, rows * own_cols), BF16),
        pltpu.VMEM((ext, K, BAND), F32),
        pltpu.VMEM((ext, K, BAND), F32),
        pltpu.VMEM((2, C, C), F32),
        pltpu.VMEM((K, half, C), F32),
        pltpu.VMEM((K, half, C), BF16),
        pltpu.VMEM((K, half, C), BF16),
        pltpu.VMEM((3, K, half // 4, C), BF16),
        pltpu.VMEM((3, K, half // 4, C), BF16),
        pltpu.VMEM((K, half // 4, C), F32),
        pltpu.VMEM((3, 2, half // 4, C), BF16),
        pltpu.VMEM((3, 2, half // 4, C), BF16),
        pltpu.VMEM((2, half // 4, C), F32),
        pltpu.VMEM((3, half // 8, C), F32),
        dma((4,)),
        dma((2, 12)), dma((2, 12)),
        dma((K // 2,)), dma((K // 2,)),
        dma((3, K // 2)), dma((3, K // 2)),
        dma((3,)), dma((3,)),
        dma((3,)), dma((3,)),
    ]
    output, grad_inputs, grad_weight = pl.pallas_call(
        kernel,
        out_shape=(
            jax.ShapeDtypeStruct(inputs.shape, BF16),
            jax.ShapeDtypeStruct(inputs.shape, BF16),
            jax.ShapeDtypeStruct((half // 8, C), F32),
        ),
        in_specs=[anywhere] * 4,
        out_specs=(vmem, vmem, vmem),
        scratch_shapes=scratch,
        compiler_params=pltpu.CompilerParams(
            collective_id=0, has_side_effects=True, vmem_limit_bytes=60 * 2**20),
    )(cotangent, inputs, taps, weight)
    return output, grad_inputs, grad_weight


def solution(mesh):
    in_specs = (P("lat", "lon", None), P(), P(), P(), P("lat", "lon", None))
    out_specs = (P("lat", "lon", None), P("lat", "lon", None), P(("lon", "lat"), None))
    return jax.shard_map(shards, mesh=mesh, in_specs=in_specs, out_specs=out_specs, check_vma=False)
```

```python
import functools
import math

import jax
import jax.numpy as jnp
from jax import lax
from jax.experimental import pallas as pl
from jax.experimental.pallas import tpu as pltpu
from jax.sharding import PartitionSpec as P

RR = 2
SMAX = 45
REACH = 2 * RR + 1
TAPS = 2 * SMAX + 1
B = 48
W = 144
LEAD = 3
BAND = 768
MESH = pl.DeviceIdType.MESH
F32 = jnp.float32
BF16 = jnp.bfloat16


def dot(a, b):
    return jnp.dot(a, b, preferred_element_type=F32)


def kernel(
    spans, cot_hbm, x_hbm, basis_hbm, weight_hbm,
    out_ref, gin_ref, gw_ref,
    wc, wx, own_c, own_x, sl_c, sl_x, rst_c, rst_x, relay_c, relay_x, flat,
    bands, feat, weight, weight_t, xt, basis, basis_f, column, turned, near, taps, rtaps,
    tmp, gown, cs, cr, rs, rr, xs, xr, s2, ys, yr, s3, zr,
    load_sem, hs_send, hs_recv, cs_send, cs_recv, rs_send, rs_recv, xs_send, xs_recv,
    ys_send, ys_recv, zs_send, zs_recv,
):
    cols, rows, C = x_hbm.shape
    K = weight_hbm.shape[0] // C
    tiles = C // 128
    lon, lat = lax.axis_index("lon"), lax.axis_index("lat")
    nlon, nlat = lax.axis_size("lon"), lax.axis_size("lat")
    core, zl, y = lon % 2, (lon // 2) % 2, lon // 4
    x, zh = lat % 4, lat // 4
    right, left = lax.rem(lon + 1, nlon), lax.rem(lon + nlon - 1, nlon)
    not_first, not_last = lat > 0, lat < nlat - 1

    def at(lon_, lat_):
        return {"lon": lon_, "lat": lat_}

    def lon_of(y_, zl_, core_):
        return (y_ * 2 + zl_) * 2 + core_

    core_dev = at(lon_of(y, zl, 1 - core), lat)
    x_devs = [at(lon, zh * 4 + (x + d) % 4) for d in (1, 3)]
    y_devs = [at(lon_of((y + d) % 4, zl, core), lat) for d in (1, 2, 3)]
    z_steps = ((0, 1), (1, 0), (1, 1))
    z_devs = [
        at(lon_of(y, (zl + a) % 2, core), ((zh + b) % 2) * 4 + x) for a, b in z_steps
    ]

    loads = [
        pltpu.make_async_copy(cot_hbm, gin_ref, load_sem.at[0]),
        pltpu.make_async_copy(x_hbm, out_ref, load_sem.at[1]),
        pltpu.make_async_copy(basis_hbm, basis, load_sem.at[2]),
        pltpu.make_async_copy(weight_hbm, weight, load_sem.at[3]),
    ]
    for load in loads:
        load.start()

    barrier = pltpu.get_barrier_semaphore()

    def greet(device):
        pl.semaphore_signal(barrier, inc=1, device_id=device, device_id_type=MESH)

    for device in [at(left, lat), at(right, lat), core_dev] + x_devs + y_devs + z_devs:
        greet(device)

    pl.when(not_first)(lambda: greet(at(lon, lat - 1)))
    pl.when(not_last)(lambda: greet(at(lon, lat + 1)))

    chunks = ((0, 8), (8, 4), (12, 4))

    def halo(t, own, sl, w, rst, relay):
        plan = []
        for start, n in chunks:
            plan.append((sl.at[pl.ds(start, n)],
                         w.at[pl.ds(RR + start, n), pl.ds(0, B), pl.ds(0, C)],
                         at(right, lat), None, None))
        for start, n in chunks:
            plan.append((own.at[pl.ds(start, n), pl.ds(0, B)],
                         rst.at[pl.ds(RR + start, n)], at(left, lat), None, None))
        low, high = pl.ds(0, RR), pl.ds(rows - RR, RR)
        above, below = pl.ds(0, RR), pl.ds(rows + RR, RR)
        for src, dst, step, here, there in (
            (high, above, 1, not_last, not_first), (low, below, -1, not_first, not_last)
        ):
            plan.append((own.at[src], w.at[dst, pl.ds(0, 2 * B), pl.ds(C, C)],
                         at(lon, lat + step), here, there))
        for n, dst, here in ((0, above, not_first), (1, below, not_last)):
            plan.append((relay.at[n], w.at[dst, pl.ds(0, B), pl.ds(0, C)],
                         at(right, lat), here, here))
            plan.append((w.at[dst, pl.ds(0, B), pl.ds(C, C)], rst.at[dst],
                         at(left, lat), here, here))
        return [
            (pltpu.make_async_remote_copy(
                src_ref=src, dst_ref=dst, send_sem=hs_send.at[t, i],
                recv_sem=hs_recv.at[t, i], device_id=device, device_id_type=MESH),
             here, there)
            for i, (src, dst, device, here, there) in enumerate(plan)
        ]

    halo_c = halo(0, own_c, sl_c, wc, rst_c, relay_c)
    halo_x = halo(1, own_x, sl_x, wx, rst_x, relay_x)

    def guarded(condition, action):
        if condition is None:
            action()
        else:
            pl.when(condition)(action)

    def start(plan, indices):
        for i in indices:
            guarded(plan[i][1], plan[i][0].start)

    def arrive(plan, indices):
        for i in indices:
            guarded(plan[i][2], plan[i][0].wait_recv)

    def sent(plan, indices):
        for i in indices:
            guarded(plan[i][1], plan[i][0].wait_send)

    def stage(raw, own, sl):
        def widen(j, _):
            ten = pl.ds(pl.multiple_of(j * 10 * rows, 8), 10 * rows)
            block = raw[pl.ds(j * 10, 10)].reshape(10 * rows, C).astype(F32)
            for n in range(tiles):
                flat[n, ten] = block[:, n * 128:(n + 1) * 128]
            return 0
        lax.fori_loop(0, cols // 10, widen, 0)

        def step(p, _):
            for n in range(tiles):
                at_n = pl.ds(n * 128, 128)
                own[p, 0:cols, at_n] = flat[n, pl.ds(p, cols, stride=rows)].astype(BF16)
                sl[p, :, at_n] = (
                    flat[n, pl.ds((cols - B) * rows + p, B, stride=rows)].astype(BF16))
            own[p, cols:2 * B] = jnp.zeros((2 * B - cols, C), BF16)
            return 0
        lax.fori_loop(0, rows, step, 0)

    def pass_on(plan, w, relay):
        def one(n, first):
            arrive(plan, (6 + n,))
            relay[n] = w[first:first + RR, cols - B:cols, C:2 * C]
            for i in (8 + 2 * n, 9 + 2 * n):
                plan[i][0].start()
        pl.when(not_first)(lambda: one(0, 0))
        pl.when(not_last)(lambda: one(1, rows + RR))

    def place(own, w):
        def step(p, _):
            w[p + RR, B:B + cols, 0:C] = own[p, 0:cols]
            w[p + RR, 0:2 * B, C:2 * C] = own[p]
            return 0
        lax.fori_loop(0, rows, step, 0)

        def pad(p, _):
            w[p, B + cols:W, C:2 * C] = jnp.zeros((W - B - cols, C), BF16)
            return 0
        lax.fori_loop(0, rows + 2 * RR, pad, 0)

        def clear(first):
            for p in range(RR):
                w[first + p] = jnp.zeros((W, 2 * C), BF16)

        pl.when(lat == 0)(lambda: clear(0))
        pl.when(lat == nlat - 1)(lambda: clear(rows + RR))

    def right_edge(first, n, w, rst):
        def step(j, _):
            p = first + j
            r = rst[p]
            w[p, cols:cols + B, C:2 * C] = r
            w[p, B + cols:W, 0:C] = r[0:W - B - cols]
            return 0
        lax.fori_loop(0, n, step, 0)

    def outer_rows(first, w, rst):
        for p in range(RR):
            w[first + p, B:B + cols, 0:C] = w[first + p, 0:cols, C:2 * C]
        right_edge(first, RR, w, rst)

    def build_band(row_taps, i):
        for k in range(K):
            v = jnp.broadcast_to(row_taps[k:k + 1], (B, BAND))
            v = pltpu.roll(v, 0, 1, stride=1, stride_axis=0)
            bands[i, k * B:(k + 1) * B] = v.astype(BF16)

    def convolve(plan, w, rst, before):
        def group(g, _):
            for n, (first, count) in enumerate(chunks):
                @pl.when(g == n)
                def _():
                    before(n)
                    arrive(plan, (n, 3 + n))
                    right_edge(RR + first, count, w, rst)

            @pl.when(g == len(chunks))
            def _():
                before(len(chunks))
                arrive(plan, (8, 9, 10, 11))
                pl.when(not_first)(lambda: outer_rows(0, w, rst))
                pl.when(not_last)(lambda: outer_rows(rows + RR, w, rst))

            for u in range(4):
                outer = u if u < RR else rows - 4 + u
                i = jnp.where(g < len(chunks), RR + 4 * g + u, outer)
                window = w[pl.ds(i, REACH)].reshape(REACH * W, 2 * C)
                acc = dot(bands[i, :, 0:REACH * W], window).astype(BF16)
                for k in range(K):
                    for b in range(2):
                        place_at = pl.ds(pl.multiple_of(i * 2 * B + b * B, 16), B)
                        feat[place_at, k * C:(k + 1) * C] = (
                            acc[k * B:(k + 1) * B, b * C:(b + 1) * C])
            return 0
        lax.fori_loop(0, len(chunks) + 1, group, 0)

    loads[0].wait()
    stage(gin_ref, own_c, sl_c)
    pl.semaphore_wait(
        barrier, 11 + jnp.where(not_first, 1, 0) + jnp.where(not_last, 1, 0))
    start(halo_c, (6, 7, 0, 3, 1, 4))
    place(own_c, wc)

    loads[2].wait()
    basis_f[...] = basis[...].astype(F32).reshape(basis_f.shape)
    column[...] = jnp.zeros(column.shape, F32)
    turned[...] = jnp.zeros(turned.shape, F32)
    first_row = lat * rows
    for k in range(K):
        for a in range(REACH):
            column[a * W + LEAD:a * W + LEAD + TAPS] = (
                basis_f[pl.ds(a * TAPS * K + k, TAPS, stride=K)])
        turned[8:8 + nlat * rows] = column[...].T
        for n in range(BAND // 128):
            near[n, pl.ds(k, 2 * rows, stride=K)] = turned[
                pl.ds(pl.multiple_of(first_row, 8), 2 * rows), n * 128:(n + 1) * 128]
    lane = lax.broadcasted_iota(jnp.int32, (K, BAND), 1)
    away = jnp.abs(lax.rem(lane, W) - LEAD - SMAX)

    def mask_row(e, _):
        row = jnp.clip(first_row + e - RR, 0, nlat * rows - 1)
        at_e = pl.ds(pl.multiple_of((e + 8 - RR) * K, 8), K)
        v = jnp.concatenate([near[n, at_e] for n in range(BAND // 128)], axis=1)
        taps[e] = jnp.where(away <= spans[row], v, 0.0)
        return 0
    lax.fori_loop(0, rows + 2 * RR, mask_row, 0)

    pass_on(halo_c, wc, relay_c)

    flip = (lax.broadcasted_iota(jnp.int32, (BAND, BAND), 0)
            + lax.broadcasted_iota(jnp.int32, (BAND, BAND), 1))
    flip = jnp.where(flip == (REACH - 1) * W + 2 * B, 1.0, 0.0).astype(BF16)
    rtaps[...] = dot(
        taps[...].reshape((rows + 2 * RR) * K, BAND).astype(BF16), flip
    ).reshape(rows + 2 * RR, K, BAND)
    def reverse_band(i, _):
        v = rtaps[i]
        for a in range(1, REACH):
            v = jnp.where(lane >= a * W, rtaps[i + a], v)
        build_band(v, i)
        return 0
    lax.fori_loop(0, rows, reverse_band, 0)

    def turn(k, _):
        at_k = pl.ds(pl.multiple_of(k * C, C), C)
        weight_t[at_k] = weight[at_k].T
        return 0

    def while_adjoint(n):
        if n == 0:
            start(halo_c, (2, 5))
        elif n == 1:
            loads[1].wait()
            stage(out_ref, own_x, sl_x)
            place(own_x, wx)
        elif n == 2:
            loads[3].wait()
            lax.fori_loop(0, K, turn, 0)
            for g in range(4):
                xt[:, g * C:(g + 1) * C] = own_x[4 * g:4 * g + 4].reshape(C, C).T
        else:
            start(halo_x, (6, 7, 0, 3, 1, 4, 2, 5))

    convolve(halo_c, wc, rst_c, while_adjoint)
    pass_on(halo_x, wx, relay_x)

    def core_copy(j):
        two = pl.ds(2 * j, 2)
        return pltpu.make_async_remote_copy(
            src_ref=cs.at[two], dst_ref=cr.at[two], send_sem=cs_send.at[j],
            recv_sem=cs_recv.at[j], device_id=core_dev, device_id_type=MESH)

    def relay_copy(j, h):
        k = 2 * j + h
        return pltpu.make_async_remote_copy(
            src_ref=rs.at[k], dst_ref=rr.at[k], send_sem=rs_send.at[j, h],
            recv_sem=rs_recv.at[j, h], device_id=x_devs[h], device_id_type=MESH)

    def x_copy(d, j):
        two = pl.ds(2 * j, 2)
        return pltpu.make_async_remote_copy(
            src_ref=xs.at[d, two], dst_ref=xr.at[d, two], send_sem=xs_send.at[d, j],
            recv_sem=xs_recv.at[d, j], device_id=x_devs[d], device_id_type=MESH)

    def quarter(k, x_):
        return jnp.concatenate(
            [gown[k, pl.ds(pl.multiple_of(x_ * 24, 8), 24)],
             gown[k, pl.ds(pl.multiple_of(96 + x_ * 24, 8), 24)]], axis=0)

    def opposite_stage(j):
        core_copy(j).wait_recv()
        for h in range(2):
            k = 2 * j + h
            gown[k] = gown[k] + cr[k].astype(F32)
            rs[k] = quarter(k, (x + 2) % 4).astype(BF16)
            relay_copy(j, h).start()

    def x_stage(j):
        for h in range(2):
            k = 2 * j + h
            relay_copy(j, h).wait_recv()
            for d, step in enumerate((1, 3)):
                share = quarter(k, (x + step) % 4)
                if d == h:
                    share = share + rr[k].astype(F32)
                xs[d, k] = share.astype(BF16)
        for d in range(2):
            x_copy(d, j).start()

    half = C // 2

    def grad_pair(j, _):
        acc = dot(xt[...], feat[:, pl.ds(pl.multiple_of(j * 2 * C, 2 * C), 2 * C)])
        for u in range(4):
            build_band(taps[RR + 4 * j + u], 4 * j + u)
        for h in range(2):
            tmp[h] = acc[:, h * C:(h + 1) * C]
        for h in range(2):
            k = 2 * j + h
            gown[k] = tmp[h, pl.ds(pl.multiple_of(core * half, half), half)]
            cs[k] = tmp[h, pl.ds(pl.multiple_of((1 - core) * half, half), half)].astype(BF16)
        core_copy(j).start()
        pl.when(j > 0)(lambda: opposite_stage(j - 1))
        pl.when(j > 1)(lambda: x_stage(j - 2))
        return 0
    lax.fori_loop(0, K // 2, grad_pair, 0)

    def mix(matrix, result, between):
        per = rows // 2

        def step(j, _):
            pl.when(j == 1)(between)
            m = per * 2 * B
            acc = dot(feat[pl.ds(pl.multiple_of(j * m, 16), m)], matrix[...])
            for i in range(per):
                for n in range(tiles):
                    flat[n, pl.ds(j * per + i, cols, stride=rows)] = (
                        acc[i * 2 * B:i * 2 * B + cols, n * 128:(n + 1) * 128])
            return 0
        lax.fori_loop(0, 2, step, 0)

        def narrow(j, _):
            ten = pl.ds(pl.multiple_of(j * 10 * rows, 8), 10 * rows)
            block = jnp.concatenate([flat[n, ten] for n in range(tiles)], axis=1)
            result[pl.ds(j * 10, 10)] = block.astype(BF16).reshape(10, rows, C)
            return 0
        lax.fori_loop(0, cols // 10, narrow, 0)

    def during_mix():
        opposite_stage(K // 2 - 1)
        x_stage(K // 2 - 2)

    mix(weight_t, gin_ref, during_mix)
    x_stage(K // 2 - 1)

    def y_copy(d):
        return pltpu.make_async_remote_copy(
            src_ref=ys.at[d], dst_ref=yr.at[d], send_sem=ys_send.at[d],
            recv_sem=ys_recv.at[d], device_id=y_devs[d], device_id_type=MESH)

    def add_x(k, _):
        s2[k] = quarter(k, x) + xr[0, k].astype(F32) + xr[1, k].astype(F32)
        return 0

    def y_stage():
        for j in range(K // 2):
            for d in range(2):
                x_copy(d, j).wait_recv()
        lax.fori_loop(0, K, add_x, 0)
        for d in range(3):
            ys[d] = s2[pl.ds(((y + d + 1) % 4) * 2, 2)].astype(BF16)
            y_copy(d).start()

    convolve(halo_x, wx, rst_x, lambda n: y_stage() if n == 2 else None)

    def z_copy(d):
        a, b = z_steps[d]
        src = s3.at[(zl + a) % 2, pl.ds(pl.multiple_of(((zh + b) % 2) * 24, 8), 24)]
        return pltpu.make_async_remote_copy(
            src_ref=src, dst_ref=zr.at[d], send_sem=zs_send.at[d],
            recv_sem=zs_recv.at[d], device_id=z_devs[d], device_id_type=MESH)

    for d in range(3):
        y_copy(d).wait_recv()
    s3[...] = s2[pl.ds(y * 2, 2)] + sum(yr[d].astype(F32) for d in range(3))
    for d in range(3):
        z_copy(d).start()

    mix(weight, out_ref, lambda: None)

    for d in range(3):
        z_copy(d).wait_recv()
    total = s3[zl, pl.ds(pl.multiple_of(zh * 24, 8), 24)] + sum(zr[d] for d in range(3))
    scale = 1.0 / math.sqrt(rows * nlat * cols * nlon)
    gw_ref[...] = total * scale

    for plan in (halo_c, halo_x):
        sent(plan, range(12))
    for j in range(K // 2):
        core_copy(j).wait_send()
        for d in range(2):
            relay_copy(j, d).wait_send()
            x_copy(d, j).wait_send()
    for d in range(3):
        y_copy(d).wait_send()
        z_copy(d).wait_send()


def hand_over(*refs):
    n = len(refs) // 2
    for i in range(n):
        refs[n + i][...] = refs[i][...]


def shards(inputs, basis, spans, weight, cotangent):
    rows, cols, C = inputs.shape
    K = weight.shape[0] // C
    nrows = basis.shape[0]
    by_lon = (1, 0, 2)
    ext = rows + 2 * RR
    vmem = pl.BlockSpec(memory_space=pltpu.VMEM)
    anywhere = pl.BlockSpec(memory_space=pl.ANY)
    own_cols = 2 * B
    dma = pltpu.SemaphoreType.DMA
    half = C // 2
    scratch = [
        pltpu.VMEM((ext, W, 2 * C), BF16),
        pltpu.VMEM((ext, W, 2 * C), BF16),
        pltpu.VMEM((rows, own_cols, C), BF16),
        pltpu.VMEM((rows, own_cols, C), BF16),
        pltpu.VMEM((rows, B, C), BF16),
        pltpu.VMEM((rows, B, C), BF16),
        pltpu.VMEM((ext, B, C), BF16),
        pltpu.VMEM((ext, B, C), BF16),
        pltpu.VMEM((2, RR, B, C), BF16),
        pltpu.VMEM((2, RR, B, C), BF16),
        pltpu.VMEM((C // 128, cols * rows, 128), F32),
        pltpu.VMEM((rows, K * B, BAND), BF16),
        pltpu.VMEM((rows * own_cols, K * C), BF16),
        pltpu.VMEM((K * C, C), BF16),
        pltpu.VMEM((K * C, C), BF16),
        pltpu.VMEM((C, rows * own_cols), BF16),
        pltpu.VMEM((REACH, TAPS, K, nrows), BF16),
        pltpu.VMEM((REACH * TAPS * K, nrows), F32),
        pltpu.VMEM((BAND, nrows), F32),
        pltpu.VMEM((nrows + 16, BAND), F32),
        pltpu.VMEM((BAND // 128, 2 * rows * K, 128), F32),
        pltpu.VMEM((ext, K, BAND), F32),
        pltpu.VMEM((ext, K, BAND), F32),
        pltpu.VMEM((2, C, C), F32),
        pltpu.VMEM((K, half, C), F32),
        pltpu.VMEM((K, half, C), BF16),
        pltpu.VMEM((K, half, C), BF16),
        pltpu.VMEM((K, half // 4, C), BF16),
        pltpu.VMEM((K, half // 4, C), BF16),
        pltpu.VMEM((2, K, half // 4, C), BF16),
        pltpu.VMEM((2, K, half // 4, C), BF16),
        pltpu.VMEM((K, half // 4, C), F32),
        pltpu.VMEM((3, 2, half // 4, C), BF16),
        pltpu.VMEM((3, 2, half // 4, C), BF16),
        pltpu.VMEM((2, half // 4, C), F32),
        pltpu.VMEM((3, half // 8, C), F32),
        dma((4,)),
        dma((2, 12)), dma((2, 12)),
        dma((K // 2,)), dma((K // 2,)),
        dma((K // 2, 2)), dma((K // 2, 2)),
        dma((2, K // 2)), dma((2, K // 2)),
        dma((3,)), dma((3,)),
        dma((3,)), dma((3,)),
    ]
    results = pl.pallas_call(
        kernel,
        out_shape=(
            jax.ShapeDtypeStruct((cols, rows, C), BF16),
            jax.ShapeDtypeStruct((cols, rows, C), BF16),
            jax.ShapeDtypeStruct((half // 8, C), F32),
        ),
        in_specs=[pl.BlockSpec(memory_space=pltpu.SMEM)] + [anywhere] * 4,
        out_specs=(vmem, vmem, vmem),
        scratch_shapes=scratch,
        compiler_params=pltpu.CompilerParams(
            collective_id=0, has_side_effects=True, vmem_limit_bytes=60 * 2**20),
    )(spans, cotangent.transpose(by_lon), inputs.transpose(by_lon),
      basis.transpose(2, 3, 1, 0), weight)
    output, grad_inputs, grad_weight = pl.pallas_call(
        hand_over,
        out_shape=[jax.ShapeDtypeStruct(r.shape, r.dtype) for r in results],
        in_specs=[vmem] * 3,
        out_specs=[vmem] * 3,
    )(*results)
    return output.transpose(by_lon), grad_inputs.transpose(by_lon), grad_weight


def solution(mesh):
    in_specs = (P("lat", "lon", None), P(), P(), P(), P("lat", "lon", None))
    out_specs = (P("lat", "lon", None), P("lat", "lon", None), P(("lon", "lat"), None))
    return jax.shard_map(shards, mesh=mesh, in_specs=in_specs, out_specs=out_specs, check_vma=False)
```

```python
import functools
import math

import jax
import jax.numpy as jnp
from jax import lax
from jax.experimental import pallas as pl
from jax.experimental.pallas import tpu as pltpu
from jax.sharding import PartitionSpec as P

RR = 2
SMAX = 45
REACH = 2 * RR + 1
TAPS = 2 * SMAX + 1
B = 48
W = 144
LEAD = 3
BAND = 768
MESH = pl.DeviceIdType.MESH
F32 = jnp.float32
BF16 = jnp.bfloat16


def dot(a, b):
    return jnp.dot(a, b, preferred_element_type=F32)


def kernel(
    spans, cot_hbm, x_hbm, basis_hbm, weight_hbm,
    out_ref, gin_ref, gw_ref,
    wc, wx, own_c, own_x, sl_c, sl_x, rst_c, rst_x, relay_c, relay_x, flat, flat_out,
    bands, feat, weight, weight_t, xt, basis, basis_f, column, turned, near, taps, rtaps,
    tmp, gown, cs, cr, rs, rr, xs, xr, s2, ys, yr, s3, zr,
    load_sem, hs_send, hs_recv, cs_send, cs_recv, rs_send, rs_recv, xs_send, xs_recv,
    ys_send, ys_recv, zs_send, zs_recv,
):
    cols, rows, C = x_hbm.shape
    K = weight_hbm.shape[0] // C
    tiles = C // 128
    lon, lat = lax.axis_index("lon"), lax.axis_index("lat")
    nlon, nlat = lax.axis_size("lon"), lax.axis_size("lat")
    core, zl, y = lon % 2, (lon // 2) % 2, lon // 4
    x, zh = lat % 4, lat // 4
    right, left = lax.rem(lon + 1, nlon), lax.rem(lon + nlon - 1, nlon)
    not_first, not_last = lat > 0, lat < nlat - 1

    def at(lon_, lat_):
        return {"lon": lon_, "lat": lat_}

    def lon_of(y_, zl_, core_):
        return (y_ * 2 + zl_) * 2 + core_

    core_dev = at(lon_of(y, zl, 1 - core), lat)
    x_devs = [at(lon, zh * 4 + (x + d) % 4) for d in (1, 3)]
    y_devs = [at(lon_of((y + d) % 4, zl, core), lat) for d in (1, 2, 3)]
    z_steps = ((0, 1), (1, 0), (1, 1))
    z_devs = [
        at(lon_of(y, (zl + a) % 2, core), ((zh + b) % 2) * 4 + x) for a, b in z_steps
    ]

    loads = [
        pltpu.make_async_copy(cot_hbm, gin_ref, load_sem.at[0]),
        pltpu.make_async_copy(x_hbm, out_ref, load_sem.at[1]),
        pltpu.make_async_copy(basis_hbm, basis, load_sem.at[2]),
        pltpu.make_async_copy(weight_hbm, weight, load_sem.at[3]),
    ]
    for load in loads:
        load.start()

    barrier = pltpu.get_barrier_semaphore()

    def greet(device):
        pl.semaphore_signal(barrier, inc=1, device_id=device, device_id_type=MESH)

    for device in [at(left, lat), at(right, lat), core_dev] + x_devs + y_devs + z_devs:
        greet(device)

    pl.when(not_first)(lambda: greet(at(lon, lat - 1)))
    pl.when(not_last)(lambda: greet(at(lon, lat + 1)))

    chunks = ((0, 8), (8, 4), (12, 4))

    def halo(t, own, sl, w, rst, relay):
        plan = []
        for start, n in chunks:
            plan.append((sl.at[pl.ds(start, n)],
                         w.at[pl.ds(RR + start, n), pl.ds(0, B), pl.ds(0, C)],
                         at(right, lat), None, None))
        for start, n in chunks:
            plan.append((own.at[pl.ds(start, n), pl.ds(0, B)],
                         rst.at[pl.ds(RR + start, n)], at(left, lat), None, None))
        low, high = pl.ds(0, RR), pl.ds(rows - RR, RR)
        above, below = pl.ds(0, RR), pl.ds(rows + RR, RR)
        for src, dst, step, here, there in (
            (high, above, 1, not_last, not_first), (low, below, -1, not_first, not_last)
        ):
            plan.append((own.at[src], w.at[dst, pl.ds(0, 2 * B), pl.ds(C, C)],
                         at(lon, lat + step), here, there))
        for n, dst, here in ((0, above, not_first), (1, below, not_last)):
            plan.append((relay.at[n], w.at[dst, pl.ds(0, B), pl.ds(0, C)],
                         at(right, lat), here, here))
            plan.append((w.at[dst, pl.ds(0, B), pl.ds(C, C)], rst.at[dst],
                         at(left, lat), here, here))
        return [
            (pltpu.make_async_remote_copy(
                src_ref=src, dst_ref=dst, send_sem=hs_send.at[t, i],
                recv_sem=hs_recv.at[t, i], device_id=device, device_id_type=MESH),
             here, there)
            for i, (src, dst, device, here, there) in enumerate(plan)
        ]

    halo_c = halo(0, own_c, sl_c, wc, rst_c, relay_c)
    halo_x = halo(1, own_x, sl_x, wx, rst_x, relay_x)

    def guarded(condition, action):
        if condition is None:
            action()
        else:
            pl.when(condition)(action)

    def start(plan, indices):
        for i in indices:
            guarded(plan[i][1], plan[i][0].start)

    def arrive(plan, indices):
        for i in indices:
            guarded(plan[i][2], plan[i][0].wait_recv)

    def sent(plan, indices):
        for i in indices:
            guarded(plan[i][1], plan[i][0].wait_send)

    def stage(raw, own, sl):
        def widen(j, _):
            ten = pl.ds(pl.multiple_of(j * 10 * rows, 8), 10 * rows)
            block = raw[pl.ds(j * 10, 10)].reshape(10 * rows, C).astype(F32)
            for n in range(tiles):
                flat[n, ten] = block[:, n * 128:(n + 1) * 128]
            return 0
        lax.fori_loop(0, cols // 10, widen, 0)

        def step(p, _):
            for n in range(tiles):
                at_n = pl.ds(n * 128, 128)
                own[p, 0:cols, at_n] = flat[n, pl.ds(p, cols, stride=rows)].astype(BF16)
                sl[p, :, at_n] = (
                    flat[n, pl.ds((cols - B) * rows + p, B, stride=rows)].astype(BF16))
            own[p, cols:2 * B] = jnp.zeros((2 * B - cols, C), BF16)
            return 0
        lax.fori_loop(0, rows, step, 0)

    def pass_on(plan, w, relay):
        def one(n, first):
            arrive(plan, (6 + n,))
            relay[n] = w[first:first + RR, cols - B:cols, C:2 * C]
            for i in (8 + 2 * n, 9 + 2 * n):
                plan[i][0].start()
        pl.when(not_first)(lambda: one(0, 0))
        pl.when(not_last)(lambda: one(1, rows + RR))

    def place(own, w):
        def step(p, _):
            w[p + RR, B:B + cols, 0:C] = own[p, 0:cols]
            w[p + RR, 0:2 * B, C:2 * C] = own[p]
            return 0
        lax.fori_loop(0, rows, step, 0)

        def pad(p, _):
            w[p, B + cols:W, C:2 * C] = jnp.zeros((W - B - cols, C), BF16)
            return 0
        lax.fori_loop(0, rows + 2 * RR, pad, 0)

        def clear(first):
            for p in range(RR):
                w[first + p] = jnp.zeros((W, 2 * C), BF16)

        pl.when(lat == 0)(lambda: clear(0))
        pl.when(lat == nlat - 1)(lambda: clear(rows + RR))

    def right_edge(first, n, w, rst):
        def step(j, _):
            p = first + j
            r = rst[p]
            w[p, cols:cols + B, C:2 * C] = r
            w[p, B + cols:W, 0:C] = r[0:W - B - cols]
            return 0
        lax.fori_loop(0, n, step, 0)

    def outer_rows(first, w, rst):
        for p in range(RR):
            w[first + p, B:B + cols, 0:C] = w[first + p, 0:cols, C:2 * C]
        right_edge(first, RR, w, rst)

    def build_band(row_taps, i):
        for k in range(K):
            v = jnp.broadcast_to(row_taps[k:k + 1], (B, BAND))
            v = pltpu.roll(v, 0, 1, stride=1, stride_axis=0)
            bands[i, k * B:(k + 1) * B] = v.astype(BF16)

    def convolve(plan, w, rst, before):
        def group(g, _):
            for n, (first, count) in enumerate(chunks):
                @pl.when(g == n)
                def _():
                    before(n)
                    arrive(plan, (n, 3 + n))
                    right_edge(RR + first, count, w, rst)

            @pl.when(g == len(chunks))
            def _():
                before(len(chunks))
                arrive(plan, (8, 9, 10, 11))
                pl.when(not_first)(lambda: outer_rows(0, w, rst))
                pl.when(not_last)(lambda: outer_rows(rows + RR, w, rst))

            for u in range(4):
                outer = u if u < RR else rows - 4 + u
                i = jnp.where(g < len(chunks), RR + 4 * g + u, outer)
                window = w[pl.ds(i, REACH)].reshape(REACH * W, 2 * C)
                acc = dot(bands[i, :, 0:REACH * W], window).astype(BF16)
                for k in range(K):
                    for b in range(2):
                        place_at = pl.ds(pl.multiple_of(i * 2 * B + b * B, 16), B)
                        feat[place_at, k * C:(k + 1) * C] = (
                            acc[k * B:(k + 1) * B, b * C:(b + 1) * C])
            return 0
        lax.fori_loop(0, len(chunks) + 1, group, 0)

    loads[0].wait()
    stage(gin_ref, own_c, sl_c)
    pl.semaphore_wait(
        barrier, 11 + jnp.where(not_first, 1, 0) + jnp.where(not_last, 1, 0))
    start(halo_c, (6, 7, 0, 3))
    place(own_c, wc)

    loads[2].wait()
    basis_f[...] = basis[...].astype(F32).reshape(basis_f.shape)
    column[...] = jnp.zeros(column.shape, F32)
    turned[...] = jnp.zeros(turned.shape, F32)
    first_row = lat * rows
    for k in range(K):
        for a in range(REACH):
            column[a * W + LEAD:a * W + LEAD + TAPS] = (
                basis_f[pl.ds(a * TAPS * K + k, TAPS, stride=K)])
        turned[8:8 + nlat * rows] = column[...].T
        for n in range(BAND // 128):
            near[n, pl.ds(k, 2 * rows, stride=K)] = turned[
                pl.ds(pl.multiple_of(first_row, 8), 2 * rows), n * 128:(n + 1) * 128]
    lane = lax.broadcasted_iota(jnp.int32, (K, BAND), 1)
    away = jnp.abs(lax.rem(lane, W) - LEAD - SMAX)

    def mask_row(e, _):
        row = jnp.clip(first_row + e - RR, 0, nlat * rows - 1)
        at_e = pl.ds(pl.multiple_of((e + 8 - RR) * K, 8), K)
        v = jnp.concatenate([near[n, at_e] for n in range(BAND // 128)], axis=1)
        taps[e] = jnp.where(away <= spans[row], v, 0.0)
        return 0
    lax.fori_loop(0, rows + 2 * RR, mask_row, 0)

    flip = (lax.broadcasted_iota(jnp.int32, (BAND, BAND), 0)
            + lax.broadcasted_iota(jnp.int32, (BAND, BAND), 1))
    flip = jnp.where(flip == (REACH - 1) * W + 2 * B, 1.0, 0.0).astype(BF16)
    rtaps[...] = dot(
        taps[...].reshape((rows + 2 * RR) * K, BAND).astype(BF16), flip
    ).reshape(rows + 2 * RR, K, BAND)
    def reverse_band(i, _):
        v = rtaps[i]
        for a in range(1, REACH):
            v = jnp.where(lane >= a * W, rtaps[i + a], v)
        build_band(v, i)
        return 0
    lax.fori_loop(0, rows // 2, reverse_band, 0)
    start(halo_c, (1, 4))
    lax.fori_loop(rows // 2, rows, reverse_band, 0)
    start(halo_c, (2, 5))

    def turn(k, _):
        at_k = pl.ds(pl.multiple_of(k * C, C), C)
        weight_t[at_k] = weight[at_k].T
        return 0

    def while_adjoint(n):
        if n == 0:
            pass_on(halo_c, wc, relay_c)
        elif n == 1:
            loads[1].wait()
            stage(out_ref, own_x, sl_x)
            place(own_x, wx)
        elif n == 2:
            loads[3].wait()
            lax.fori_loop(0, K, turn, 0)
            for g in range(4):
                xt[:, g * C:(g + 1) * C] = own_x[4 * g:4 * g + 4].reshape(C, C).T
        elif n == 3:
            start(halo_x, (6, 7, 0, 3))

    convolve(halo_c, wc, rst_c, while_adjoint)
    start(halo_x, (1, 4))

    def core_copy(j):
        two = pl.ds(2 * j, 2)
        return pltpu.make_async_remote_copy(
            src_ref=cs.at[two], dst_ref=cr.at[two], send_sem=cs_send.at[j],
            recv_sem=cs_recv.at[j], device_id=core_dev, device_id_type=MESH)

    def relay_copy(j, h):
        k = 2 * j + h
        return pltpu.make_async_remote_copy(
            src_ref=rs.at[k], dst_ref=rr.at[k], send_sem=rs_send.at[j, h],
            recv_sem=rs_recv.at[j, h], device_id=x_devs[h], device_id_type=MESH)

    def x_copy(d, j):
        two = pl.ds(2 * j, 2)
        return pltpu.make_async_remote_copy(
            src_ref=xs.at[d, two], dst_ref=xr.at[d, two], send_sem=xs_send.at[d, j],
            recv_sem=xs_recv.at[d, j], device_id=x_devs[d], device_id_type=MESH)

    def quarter(k, x_):
        return jnp.concatenate(
            [gown[k, pl.ds(pl.multiple_of(x_ * 24, 8), 24)],
             gown[k, pl.ds(pl.multiple_of(96 + x_ * 24, 8), 24)]], axis=0)

    def opposite_stage(j):
        core_copy(j).wait_recv()
        for h in range(2):
            k = 2 * j + h
            gown[k] = gown[k] + cr[k].astype(F32)
            rs[k] = quarter(k, (x + 2) % 4).astype(BF16)
            relay_copy(j, h).start()

    def x_stage(j):
        for h in range(2):
            k = 2 * j + h
            relay_copy(j, h).wait_recv()
            for d, step in enumerate((1, 3)):
                share = quarter(k, (x + step) % 4)
                if d == h:
                    share = share + rr[k].astype(F32)
                xs[d, k] = share.astype(BF16)
        for d in range(2):
            x_copy(d, j).start()

    half = C // 2

    def grad_pair(j, _):
        acc = dot(xt[...], feat[:, pl.ds(pl.multiple_of(j * 2 * C, 2 * C), 2 * C)])
        for u in range(4):
            build_band(taps[RR + 4 * j + u], 4 * j + u)
        for h in range(2):
            tmp[h] = acc[:, h * C:(h + 1) * C]
        for h in range(2):
            k = 2 * j + h
            gown[k] = tmp[h, pl.ds(pl.multiple_of(core * half, half), half)]
            cs[k] = tmp[h, pl.ds(pl.multiple_of((1 - core) * half, half), half)].astype(BF16)
        core_copy(j).start()
        pl.when(j > 0)(lambda: opposite_stage(j - 1))
        return 0
    lax.fori_loop(0, K // 2, grad_pair, 0)
    start(halo_x, (2, 5))

    per = rows // 2
    m = per * 2 * B

    def mix(j, matrix):
        return dot(feat[j * m:(j + 1) * m], matrix[...])

    sent(halo_c, (3, 4, 5, 6, 7))
    for j in range(2):
        acc = mix(j, weight_t).astype(BF16)
        for i in range(per):
            own_c[j * per + i] = acc[i * 2 * B:(i + 1) * 2 * B]
        if j == 0:
            opposite_stage(K // 2 - 1)
            pass_on(halo_x, wx, relay_x)
    for j in range(K // 2):
        x_stage(j)


    def y_copy(d):
        return pltpu.make_async_remote_copy(
            src_ref=ys.at[d], dst_ref=yr.at[d], send_sem=ys_send.at[d],
            recv_sem=ys_recv.at[d], device_id=y_devs[d], device_id_type=MESH)

    def add_x(k, _):
        s2[k] = quarter(k, x) + xr[0, k].astype(F32) + xr[1, k].astype(F32)
        return 0

    def y_stage():
        for j in range(K // 2):
            for d in range(2):
                x_copy(d, j).wait_recv()
        lax.fori_loop(0, K, add_x, 0)
        for d in range(3):
            ys[d] = s2[pl.ds(((y + d + 1) % 4) * 2, 2)].astype(BF16)
            y_copy(d).start()

    def while_forward(n):
        if n == 3:
            y_stage()

    convolve(halo_x, wx, rst_x, while_forward)

    def z_copy(d):
        a, b = z_steps[d]
        src = s3.at[(zl + a) % 2, pl.ds(pl.multiple_of(((zh + b) % 2) * 24, 8), 24)]
        return pltpu.make_async_remote_copy(
            src_ref=src, dst_ref=zr.at[d], send_sem=zs_send.at[d],
            recv_sem=zs_recv.at[d], device_id=z_devs[d], device_id_type=MESH)

    def z_stage():
        for d in range(3):
            y_copy(d).wait_recv()
        s3[...] = s2[pl.ds(y * 2, 2)] + sum(yr[d].astype(F32) for d in range(3))
        for d in range(3):
            z_copy(d).start()

    def narrow(wide, result):
        def step(j, _):
            ten = pl.ds(pl.multiple_of(j * 10 * rows, 8), 10 * rows)
            block = jnp.concatenate([wide[n, ten] for n in range(tiles)], axis=1)
            result[pl.ds(j * 10, 10)] = block.astype(BF16).reshape(10, rows, C)
            return 0
        lax.fori_loop(0, cols // 10, step, 0, unroll=True)

    for j in range(2):
        if j == 0:
            for p in range(rows):
                for n in range(tiles):
                    flat[n, pl.ds(p, cols, stride=rows)] = (
                        own_c[p, 0:cols, n * 128:(n + 1) * 128].astype(F32))
        else:
            z_stage()
            narrow(flat, gin_ref)
        acc = mix(j, weight)
        for i in range(per):
            for n in range(tiles):
                flat_out[n, pl.ds(j * per + i, cols, stride=rows)] = (
                    acc[i * 2 * B:i * 2 * B + cols, n * 128:(n + 1) * 128])
    narrow(flat_out, out_ref)

    for d in range(3):
        z_copy(d).wait_recv()
    total = s3[zl, pl.ds(pl.multiple_of(zh * 24, 8), 24)] + sum(zr[d] for d in range(3))
    scale = 1.0 / math.sqrt(rows * nlat * cols * nlon)
    gw_ref[...] = total * scale

    for plan in (halo_c, halo_x):
        sent(plan, (0, 1, 2, 8, 9, 10, 11) + ((3, 4, 5, 6, 7) if plan is halo_x else ()))
    for j in range(K // 2):
        core_copy(j).wait_send()
        for d in range(2):
            relay_copy(j, d).wait_send()
            x_copy(d, j).wait_send()
    for d in range(3):
        y_copy(d).wait_send()
        z_copy(d).wait_send()


def hand_over(*refs):
    n = len(refs) // 2
    for i in range(n):
        refs[n + i][...] = refs[i][...]


def shards(inputs, basis, spans, weight, cotangent):
    rows, cols, C = inputs.shape
    K = weight.shape[0] // C
    nrows = basis.shape[0]
    by_lon = (1, 0, 2)
    ext = rows + 2 * RR
    vmem = pl.BlockSpec(memory_space=pltpu.VMEM)
    anywhere = pl.BlockSpec(memory_space=pl.ANY)
    own_cols = 2 * B
    dma = pltpu.SemaphoreType.DMA
    half = C // 2
    scratch = [
        pltpu.VMEM((ext, W, 2 * C), BF16),
        pltpu.VMEM((ext, W, 2 * C), BF16),
        pltpu.VMEM((rows, own_cols, C), BF16),
        pltpu.VMEM((rows, own_cols, C), BF16),
        pltpu.VMEM((rows, B, C), BF16),
        pltpu.VMEM((rows, B, C), BF16),
        pltpu.VMEM((ext, B, C), BF16),
        pltpu.VMEM((ext, B, C), BF16),
        pltpu.VMEM((2, RR, B, C), BF16),
        pltpu.VMEM((2, RR, B, C), BF16),
        pltpu.VMEM((C // 128, cols * rows, 128), F32),
        pltpu.VMEM((C // 128, cols * rows, 128), F32),
        pltpu.VMEM((rows, K * B, BAND), BF16),
        pltpu.VMEM((rows * own_cols, K * C), BF16),
        pltpu.VMEM((K * C, C), BF16),
        pltpu.VMEM((K * C, C), BF16),
        pltpu.VMEM((C, rows * own_cols), BF16),
        pltpu.VMEM((REACH, TAPS, K, nrows), BF16),
        pltpu.VMEM((REACH * TAPS * K, nrows), F32),
        pltpu.VMEM((BAND, nrows), F32),
        pltpu.VMEM((nrows + 16, BAND), F32),
        pltpu.VMEM((BAND // 128, 2 * rows * K, 128), F32),
        pltpu.VMEM((ext, K, BAND), F32),
        pltpu.VMEM((ext, K, BAND), F32),
        pltpu.VMEM((2, C, C), F32),
        pltpu.VMEM((K, half, C), F32),
        pltpu.VMEM((K, half, C), BF16),
        pltpu.VMEM((K, half, C), BF16),
        pltpu.VMEM((K, half // 4, C), BF16),
        pltpu.VMEM((K, half // 4, C), BF16),
        pltpu.VMEM((2, K, half // 4, C), BF16),
        pltpu.VMEM((2, K, half // 4, C), BF16),
        pltpu.VMEM((K, half // 4, C), F32),
        pltpu.VMEM((3, 2, half // 4, C), BF16),
        pltpu.VMEM((3, 2, half // 4, C), BF16),
        pltpu.VMEM((2, half // 4, C), F32),
        pltpu.VMEM((3, half // 8, C), F32),
        dma((4,)),
        dma((2, 12)), dma((2, 12)),
        dma((K // 2,)), dma((K // 2,)),
        dma((K // 2, 2)), dma((K // 2, 2)),
        dma((2, K // 2)), dma((2, K // 2)),
        dma((3,)), dma((3,)),
        dma((3,)), dma((3,)),
    ]
    results = pl.pallas_call(
        kernel,
        out_shape=(
            jax.ShapeDtypeStruct((cols, rows, C), BF16),
            jax.ShapeDtypeStruct((cols, rows, C), BF16),
            jax.ShapeDtypeStruct((half // 8, C), F32),
        ),
        in_specs=[pl.BlockSpec(memory_space=pltpu.SMEM)] + [anywhere] * 4,
        out_specs=(vmem, vmem, vmem),
        scratch_shapes=scratch,
        compiler_params=pltpu.CompilerParams(
            collective_id=0, has_side_effects=True, vmem_limit_bytes=62 * 2**20),
    )(spans, cotangent.transpose(by_lon), inputs.transpose(by_lon),
      basis.transpose(2, 3, 1, 0), weight)
    output, grad_inputs, grad_weight = pl.pallas_call(
        hand_over,
        out_shape=[jax.ShapeDtypeStruct(r.shape, r.dtype) for r in results],
        in_specs=[vmem] * 3,
        out_specs=[vmem] * 3,
    )(*results)
    return output.transpose(by_lon), grad_inputs.transpose(by_lon), grad_weight


def solution(mesh):
    in_specs = (P("lat", "lon", None), P(), P(), P(), P("lat", "lon", None))
    out_specs = (P("lat", "lon", None), P("lat", "lon", None), P(("lon", "lat"), None))
    return jax.shard_map(shards, mesh=mesh, in_specs=in_specs, out_specs=out_specs, check_vma=False)
```

```python
import functools
import math

import jax
import jax.numpy as jnp
from jax import lax
from jax.experimental import pallas as pl
from jax.experimental.pallas import tpu as pltpu
from jax.sharding import PartitionSpec as P

RR = 2
SMAX = 45
REACH = 2 * RR + 1
TAPS = 2 * SMAX + 1
B = 48
W = 144
LEAD = 3
BAND = 768
MESH = pl.DeviceIdType.MESH
F32 = jnp.float32
BF16 = jnp.bfloat16


def dot(a, b):
    return jnp.dot(a, b, preferred_element_type=F32)


def kernel(
    spans, cot_hbm, x_hbm, basis_hbm, weight_hbm,
    out_ref, gin_ref, gw_ref,
    wc, wx, own_c, own_x, sl_c, sl_x, rst_c, rst_x, relay_c, relay_x, flat, flat_out,
    bands, feat, weight, weight_t, xt, basis, basis_f, column, turned, near, taps, rtaps,
    tmp, gown, cs, cr, rs, rr, xs, xr, s2, ys, yr, s3, zr,
    load_sem, hs_send, hs_recv, cs_send, cs_recv, rs_send, rs_recv, xs_send, xs_recv,
    ys_send, ys_recv, zs_send, zs_recv,
):
    cols, rows, C = x_hbm.shape
    K = weight_hbm.shape[0] // C
    tiles = C // 128
    lon, lat = lax.axis_index("lon"), lax.axis_index("lat")
    nlon, nlat = lax.axis_size("lon"), lax.axis_size("lat")
    core, zl, y = lon % 2, (lon // 2) % 2, lon // 4
    x, zh = lat % 4, lat // 4
    right, left = lax.rem(lon + 1, nlon), lax.rem(lon + nlon - 1, nlon)
    not_first, not_last = lat > 0, lat < nlat - 1
    far_above = jnp.logical_and(not_first, x == 0)
    far_below = jnp.logical_and(not_last, x == 3)
    near_above = jnp.logical_and(not_first, x != 0)
    near_below = jnp.logical_and(not_last, x != 3)

    def at(lon_, lat_):
        return {"lon": lon_, "lat": lat_}

    def lon_of(y_, zl_, core_):
        return (y_ * 2 + zl_) * 2 + core_

    core_dev = at(lon_of(y, zl, 1 - core), lat)
    x_devs = [at(lon, zh * 4 + (x + d) % 4) for d in (1, 3)]
    y_devs = [at(lon_of((y + d) % 4, zl, core), lat) for d in (1, 2, 3)]
    z_steps = ((0, 1), (1, 0), (1, 1))
    z_devs = [
        at(lon_of(y, (zl + a) % 2, core), ((zh + b) % 2) * 4 + x) for a, b in z_steps
    ]

    loads = [
        pltpu.make_async_copy(cot_hbm, gin_ref, load_sem.at[0]),
        pltpu.make_async_copy(x_hbm, out_ref, load_sem.at[1]),
        pltpu.make_async_copy(basis_hbm, basis, load_sem.at[2]),
        pltpu.make_async_copy(weight_hbm, weight, load_sem.at[3]),
    ]
    for load in loads:
        load.start()

    barrier = pltpu.get_barrier_semaphore()

    def greet(device):
        pl.semaphore_signal(barrier, inc=1, device_id=device, device_id_type=MESH)

    for device in [at(left, lat), at(right, lat), core_dev] + x_devs + y_devs + z_devs:
        greet(device)

    pl.when(not_first)(lambda: greet(at(lon, lat - 1)))
    pl.when(not_last)(lambda: greet(at(lon, lat + 1)))

    chunks = ((0, 8), (8, 4), (12, 4))

    def halo(t, own, sl, w, rst, relay):
        plan = []
        for start, n in chunks:
            plan.append((sl.at[pl.ds(start, n)],
                         w.at[pl.ds(RR + start, n), pl.ds(0, B), pl.ds(0, C)],
                         at(right, lat), None, None))
        for start, n in chunks:
            plan.append((own.at[pl.ds(start, n), pl.ds(0, B)],
                         rst.at[pl.ds(RR + start, n)], at(left, lat), None, None))
        low, high = pl.ds(0, RR), pl.ds(rows - RR, RR)
        above, below = pl.ds(0, RR), pl.ds(rows + RR, RR)
        for src, dst, step, here, there in (
            (high, above, 1, not_last, not_first), (low, below, -1, not_first, not_last)
        ):
            plan.append((own.at[src], w.at[dst, pl.ds(0, 2 * B), pl.ds(C, C)],
                         at(lon, lat + step), here, there))
        for n, dst, here, there in (
            (0, above, far_above, not_first), (1, below, far_below, not_last)
        ):
            plan.append((relay.at[n], w.at[dst, pl.ds(0, B), pl.ds(0, C)],
                         at(right, lat), here, there))
            plan.append((w.at[dst, pl.ds(0, B), pl.ds(C, C)], rst.at[dst],
                         at(left, lat), here, there))
        for src, dst, step, here in (
            (pl.ds(rows, RR), above, 1, near_below), (pl.ds(RR, RR), below, -1, near_above)
        ):
            side = (pl.ds(0, B), pl.ds(0, C))
            plan.append((w.at[(src,) + side], w.at[(dst,) + side],
                         at(lon, lat + step), here, None))
            plan.append((rst.at[src], rst.at[dst], at(lon, lat + step), here, None))
        return [
            (pltpu.make_async_remote_copy(
                src_ref=src, dst_ref=dst, send_sem=hs_send.at[t, i],
                recv_sem=hs_recv.at[t, i if i < 12 else i - 4], device_id=device, device_id_type=MESH),
             here, there)
            for i, (src, dst, device, here, there) in enumerate(plan)
        ]

    halo_c = halo(0, own_c, sl_c, wc, rst_c, relay_c)
    halo_x = halo(1, own_x, sl_x, wx, rst_x, relay_x)

    def guarded(condition, action):
        if condition is None:
            action()
        else:
            pl.when(condition)(action)

    def start(plan, indices):
        for i in indices:
            guarded(plan[i][1], plan[i][0].start)

    def arrive(plan, indices):
        for i in indices:
            guarded(plan[i][2], plan[i][0].wait_recv)

    def sent(plan, indices):
        for i in indices:
            guarded(plan[i][1], plan[i][0].wait_send)

    def widen(raw):
        def step(j, _):
            ten = pl.ds(pl.multiple_of(j * 10 * rows, 8), 10 * rows)
            block = raw[pl.ds(j * 10, 10)].reshape(10 * rows, C).astype(F32)
            for n in range(tiles):
                flat[n, ten] = block[:, n * 128:(n + 1) * 128]
            return 0
        lax.fori_loop(0, cols // 10, step, 0)

    def stage(first, n_rows, own, sl):
        def step(p, _):
            for n in range(tiles):
                at_n = pl.ds(n * 128, 128)
                own[p, 0:cols, at_n] = flat[n, pl.ds(p, cols, stride=rows)].astype(BF16)
                sl[p, :, at_n] = (
                    flat[n, pl.ds((cols - B) * rows + p, B, stride=rows)].astype(BF16))
            own[p, cols:2 * B] = jnp.zeros((2 * B - cols, C), BF16)
            return 0
        lax.fori_loop(first, first + n_rows, step, 0)

    def pass_on(plan, w, relay):
        def one(n, first):
            plan[6 + n][0].wait_recv()
            relay[n] = w[first:first + RR, cols - B:cols, C:2 * C]
            for i in (8 + 2 * n, 9 + 2 * n):
                plan[i][0].start()
        pl.when(far_above)(lambda: one(0, 0))
        pl.when(far_below)(lambda: one(1, rows + RR))

    def place(own, w):
        def step(p, _):
            w[p + RR, B:B + cols, 0:C] = own[p, 0:cols]
            w[p + RR, 0:2 * B, C:2 * C] = own[p]
            return 0
        lax.fori_loop(0, rows, step, 0)

        def pad(p, _):
            w[p, B + cols:W, C:2 * C] = jnp.zeros((W - B - cols, C), BF16)
            return 0
        lax.fori_loop(0, rows + 2 * RR, pad, 0)

        def clear(first):
            for p in range(RR):
                w[first + p] = jnp.zeros((W, 2 * C), BF16)

        pl.when(lat == 0)(lambda: clear(0))
        pl.when(lat == nlat - 1)(lambda: clear(rows + RR))

    def right_edge(first, n, w, rst):
        def step(j, _):
            p = first + j
            r = rst[p]
            w[p, cols:cols + B, C:2 * C] = r
            w[p, B + cols:W, 0:C] = r[0:W - B - cols]
            return 0
        lax.fori_loop(0, n, step, 0)

    def outer_rows(first, w, rst):
        for p in range(RR):
            w[first + p, B:B + cols, 0:C] = w[first + p, 0:cols, C:2 * C]
        right_edge(first, RR, w, rst)

    def build_band(row_taps, i):
        for k in range(K):
            v = jnp.broadcast_to(row_taps[k:k + 1], (B, BAND))
            v = pltpu.roll(v, 0, 1, stride=1, stride_axis=0)
            bands[i, k * B:(k + 1) * B] = v.astype(BF16)

    def convolve(plan, w, rst, needs, before):
        def group(g, _):
            for n in range(len(chunks)):
                @pl.when(g == n)
                def _():
                    before(n)
                    for c in needs[n]:
                        arrive(plan, (c, 3 + c))
                        right_edge(RR + chunks[c][0], chunks[c][1], w, rst)
                        if c == 0:
                            start(plan, (14, 15))
                        if c == 2:
                            start(plan, (12, 13))

            @pl.when(g == len(chunks))
            def _():
                before(len(chunks))
                pl.when(near_above)(plan[6][0].wait_recv)
                pl.when(near_below)(plan[7][0].wait_recv)
                arrive(plan, (8, 9, 10, 11))
                pl.when(not_first)(lambda: outer_rows(0, w, rst))
                pl.when(not_last)(lambda: outer_rows(rows + RR, w, rst))

            for u in range(4):
                outer = u if u < RR else rows - 4 + u
                i = jnp.where(g < len(chunks), RR + 4 * g + u, outer)
                window = w[pl.ds(i, REACH)].reshape(REACH * W, 2 * C)
                acc = dot(bands[i, :, 0:REACH * W], window).astype(BF16)
                for k in range(K):
                    for b in range(2):
                        place_at = pl.ds(pl.multiple_of(i * 2 * B + b * B, 16), B)
                        feat[place_at, k * C:(k + 1) * C] = (
                            acc[k * B:(k + 1) * B, b * C:(b + 1) * C])
            return 0
        lax.fori_loop(0, len(chunks) + 1, group, 0)

    loads[0].wait()
    widen(gin_ref)
    stage(0, 8, own_c, sl_c)
    pl.semaphore_wait(
        barrier, 11 + jnp.where(not_first, 1, 0) + jnp.where(not_last, 1, 0))
    start(halo_c, (0, 3, 7))
    stage(8, 8, own_c, sl_c)
    start(halo_c, (6,))
    place(own_c, wc)

    loads[2].wait()
    basis_f[...] = basis[...].astype(F32).reshape(basis_f.shape)
    column[...] = jnp.zeros(column.shape, F32)
    turned[...] = jnp.zeros(turned.shape, F32)
    first_row = lat * rows
    for k in range(K):
        for a in range(REACH):
            column[a * W + LEAD:a * W + LEAD + TAPS] = (
                basis_f[pl.ds(a * TAPS * K + k, TAPS, stride=K)])
        turned[8:8 + nlat * rows] = column[...].T
        for n in range(BAND // 128):
            near[n, pl.ds(k, 2 * rows, stride=K)] = turned[
                pl.ds(pl.multiple_of(first_row, 8), 2 * rows), n * 128:(n + 1) * 128]
    lane = lax.broadcasted_iota(jnp.int32, (K, BAND), 1)
    away = jnp.abs(lax.rem(lane, W) - LEAD - SMAX)

    def mask_row(e, _):
        row = jnp.clip(first_row + e - RR, 0, nlat * rows - 1)
        at_e = pl.ds(pl.multiple_of((e + 8 - RR) * K, 8), K)
        v = jnp.concatenate([near[n, at_e] for n in range(BAND // 128)], axis=1)
        taps[e] = jnp.where(away <= spans[row], v, 0.0)
        return 0
    lax.fori_loop(0, rows + 2 * RR, mask_row, 0)

    flip = (lax.broadcasted_iota(jnp.int32, (128, 128), 0)
            + lax.broadcasted_iota(jnp.int32, (128, 128), 1))
    flip = jnp.where(flip == 127, 1.0, 0.0).astype(BF16)
    every = taps[...].reshape((rows + 2 * RR) * K, BAND).astype(BF16)
    last = BAND // 128 - 1
    every = jnp.concatenate(
        [dot(every[:, (last - n) * 128:(last - n + 1) * 128], flip)
         for n in range(last + 1)], axis=1)
    every = pltpu.roll(every, (REACH - 1) * W + 2 * B + 1, 1)
    rtaps[...] = every.reshape(rows + 2 * RR, K, BAND)

    def reverse_band(i, _):
        v = rtaps[i]
        for a in range(1, REACH):
            v = jnp.where(lane >= a * W, rtaps[i + a], v)
        build_band(v, i)
        return 0
    lax.fori_loop(0, rows // 2, reverse_band, 0)
    start(halo_c, (1, 4))
    lax.fori_loop(rows // 2, rows, reverse_band, 0)
    start(halo_c, (2, 5))

    def turn(k, _):
        at_k = pl.ds(pl.multiple_of(k * C, C), C)
        weight_t[at_k] = weight[at_k].T
        return 0

    def while_adjoint(n):
        if n == 0:
            pass_on(halo_c, wc, relay_c)
        elif n == 1:
            loads[1].wait()
            widen(out_ref)
            stage(0, 8, own_x, sl_x)
        elif n == 2:
            stage(8, 8, own_x, sl_x)
            place(own_x, wx)
            for g in range(4):
                xt[:, g * C:(g + 1) * C] = own_x[4 * g:4 * g + 4].reshape(C, C).T
        elif n == 3:
            start(halo_x, (6, 7, 0, 3))
            loads[3].wait()
            lax.fori_loop(0, K, turn, 0)

    convolve(halo_c, wc, rst_c, ((0,), (1,), (2,)), while_adjoint)
    start(halo_x, (1, 4))

    part = K // 2

    def core_copy(j):
        these = pl.ds(part * j, part)
        return pltpu.make_async_remote_copy(
            src_ref=cs.at[these], dst_ref=cr.at[these], send_sem=cs_send.at[j],
            recv_sem=cs_recv.at[j], device_id=core_dev, device_id_type=MESH)

    def relay_copy(j, h):
        these = pl.ds(part // 2 * j, part // 2)
        return pltpu.make_async_remote_copy(
            src_ref=rs.at[h, these], dst_ref=rr.at[h, these], send_sem=rs_send.at[j, h],
            recv_sem=rs_recv.at[j, h], device_id=x_devs[h], device_id_type=MESH)

    def x_copy(d, j):
        these = pl.ds(part * j, part)
        return pltpu.make_async_remote_copy(
            src_ref=xs.at[d, these], dst_ref=xr.at[d, these], send_sem=xs_send.at[d, j],
            recv_sem=xs_recv.at[d, j], device_id=x_devs[d], device_id_type=MESH)

    def quarter(k, x_):
        return jnp.concatenate(
            [gown[k, pl.ds(pl.multiple_of(x_ * 24, 8), 24)],
             gown[k, pl.ds(pl.multiple_of(96 + x_ * 24, 8), 24)]], axis=0)

    def opposite_stage(j):
        core_copy(j).wait_recv()
        for k in range(part * j, part * (j + 1)):
            gown[k] = gown[k] + cr[k].astype(F32)
            rs[k % 2, k // 2] = quarter(k, (x + 2) % 4).astype(BF16)
        for h in range(2):
            relay_copy(j, h).start()

    def x_stage(j):
        for h in range(2):
            relay_copy(j, h).wait_recv()
        for k in range(part * j, part * (j + 1)):
            for d, step in enumerate((1, 3)):
                share = quarter(k, (x + step) % 4)
                if d == k % 2:
                    share = share + rr[k % 2, k // 2].astype(F32)
                xs[d, k] = share.astype(BF16)
        for d in range(2):
            x_copy(d, j).start()

    half = C // 2

    def grad_pair(j, _):
        acc = dot(xt[...], feat[:, pl.ds(pl.multiple_of(j * 2 * C, 2 * C), 2 * C)])
        for u in range(4):
            build_band(taps[RR + 4 * j + u], 4 * j + u)
        for h in range(2):
            tmp[h] = acc[:, h * C:(h + 1) * C]
        for h in range(2):
            k = 2 * j + h
            gown[k] = tmp[h, pl.ds(pl.multiple_of(core * half, half), half)]
            cs[k] = tmp[h, pl.ds(pl.multiple_of((1 - core) * half, half), half)].astype(BF16)
        pl.when(j == 1)(lambda: core_copy(0).start())

        @pl.when(j == 3)
        def _():
            core_copy(1).start()
            opposite_stage(0)
        return 0
    lax.fori_loop(0, K // 2, grad_pair, 0)
    start(halo_x, (2, 5))

    per = rows // 2
    m = per * 2 * B

    def mix(j, matrix):
        return dot(feat[j * m:(j + 1) * m], matrix[...])

    sent(halo_c, (3, 4, 5, 6, 7))
    for j in range(2):
        acc = mix(j, weight_t).astype(BF16)
        for i in range(per):
            own_c[j * per + i] = acc[i * 2 * B:(i + 1) * 2 * B]
        if j == 0:
            opposite_stage(1)
            x_stage(0)
            pass_on(halo_x, wx, relay_x)
    x_stage(1)


    def y_copy(d):
        return pltpu.make_async_remote_copy(
            src_ref=ys.at[d], dst_ref=yr.at[d], send_sem=ys_send.at[d],
            recv_sem=ys_recv.at[d], device_id=y_devs[d], device_id_type=MESH)

    def add_x(k, _):
        s2[k] = quarter(k, x) + xr[0, k].astype(F32) + xr[1, k].astype(F32)
        return 0

    def y_stage():
        for j in range(2):
            for d in range(2):
                x_copy(d, j).wait_recv()
        lax.fori_loop(0, K, add_x, 0)
        for d in range(3):
            ys[d] = s2[pl.ds(((y + d + 1) % 4) * 2, 2)].astype(BF16)
            y_copy(d).start()

    def while_forward(n):
        if n == 2:
            y_stage()

    convolve(halo_x, wx, rst_x, ((0, 1), (2,), ()), while_forward)

    def z_copy(d):
        a, b = z_steps[d]
        src = s3.at[(zl + a) % 2, pl.ds(pl.multiple_of(((zh + b) % 2) * 24, 8), 24)]
        return pltpu.make_async_remote_copy(
            src_ref=src, dst_ref=zr.at[d], send_sem=zs_send.at[d],
            recv_sem=zs_recv.at[d], device_id=z_devs[d], device_id_type=MESH)

    def z_stage():
        for d in range(3):
            y_copy(d).wait_recv()
        s3[...] = s2[pl.ds(y * 2, 2)] + sum(yr[d].astype(F32) for d in range(3))
        for d in range(3):
            z_copy(d).start()

    def narrow(wide, result):
        def step(j, _):
            ten = pl.ds(pl.multiple_of(j * 10 * rows, 8), 10 * rows)
            block = jnp.concatenate([wide[n, ten] for n in range(tiles)], axis=1)
            result[pl.ds(j * 10, 10)] = block.astype(BF16).reshape(10, rows, C)
            return 0
        lax.fori_loop(0, cols // 10, step, 0, unroll=True)

    for j in range(2):
        if j == 0:
            for p in range(rows):
                for n in range(tiles):
                    flat[n, pl.ds(p, cols, stride=rows)] = (
                        own_c[p, 0:cols, n * 128:(n + 1) * 128].astype(F32))
        else:
            z_stage()
            narrow(flat, gin_ref)
        acc = mix(j, weight)
        for i in range(per):
            for n in range(tiles):
                flat_out[n, pl.ds(j * per + i, cols, stride=rows)] = (
                    acc[i * 2 * B:i * 2 * B + cols, n * 128:(n + 1) * 128])
    narrow(flat_out, out_ref)

    for d in range(3):
        z_copy(d).wait_recv()
    total = s3[zl, pl.ds(pl.multiple_of(zh * 24, 8), 24)] + sum(zr[d] for d in range(3))
    scale = 1.0 / math.sqrt(rows * nlat * cols * nlon)
    gw_ref[...] = total * scale

    for plan in (halo_c, halo_x):
        sent(plan, (0, 1, 2, 8, 9, 10, 11, 12, 13, 14, 15) + ((3, 4, 5, 6, 7) if plan is halo_x else ()))
    for j in range(2):
        core_copy(j).wait_send()
        for d in range(2):
            relay_copy(j, d).wait_send()
            x_copy(d, j).wait_send()
    for d in range(3):
        y_copy(d).wait_send()
        z_copy(d).wait_send()


def hand_over(out, gin, gw, out_to, gin_to, gw_to, out_v, gin_v, gw_v, sem_in, sem_out):
    parts = 3
    n = out.shape[0] // parts
    moves = []
    for i in range(parts):
        piece = pl.ds(i * n, n)
        moves.append((out.at[piece], out_v.at[piece], out_to.at[piece]))
        moves.append((gin.at[piece], gin_v.at[piece], gin_to.at[piece]))
    moves.append((gw, gw_v, gw_to))
    arriving = [
        pltpu.make_async_copy(a, b, sem_in.at[i]) for i, (a, b, _) in enumerate(moves)]
    leaving = [
        pltpu.make_async_copy(b, c, sem_out.at[i]) for i, (_, b, c) in enumerate(moves)]
    for copy in arriving:
        copy.start()
    for first, second in zip(arriving, leaving):
        first.wait()
        second.start()
    for copy in leaving:
        copy.wait()


def shards(inputs, basis, spans, weight, cotangent):
    rows, cols, C = inputs.shape
    K = weight.shape[0] // C
    nrows = basis.shape[0]
    by_lon = (1, 0, 2)
    ext = rows + 2 * RR
    vmem = pl.BlockSpec(memory_space=pltpu.VMEM)
    anywhere = pl.BlockSpec(memory_space=pl.ANY)
    own_cols = 2 * B
    dma = pltpu.SemaphoreType.DMA
    half = C // 2
    scratch = [
        pltpu.VMEM((ext, W, 2 * C), BF16),
        pltpu.VMEM((ext, W, 2 * C), BF16),
        pltpu.VMEM((rows, own_cols, C), BF16),
        pltpu.VMEM((rows, own_cols, C), BF16),
        pltpu.VMEM((rows, B, C), BF16),
        pltpu.VMEM((rows, B, C), BF16),
        pltpu.VMEM((ext, B, C), BF16),
        pltpu.VMEM((ext, B, C), BF16),
        pltpu.VMEM((2, RR, B, C), BF16),
        pltpu.VMEM((2, RR, B, C), BF16),
        pltpu.VMEM((C // 128, cols * rows, 128), F32),
        pltpu.VMEM((C // 128, cols * rows, 128), F32),
        pltpu.VMEM((rows, K * B, BAND), BF16),
        pltpu.VMEM((rows * own_cols, K * C), BF16),
        pltpu.VMEM((K * C, C), BF16),
        pltpu.VMEM((K * C, C), BF16),
        pltpu.VMEM((C, rows * own_cols), BF16),
        pltpu.VMEM((REACH, TAPS, K, nrows), BF16),
        pltpu.VMEM((REACH * TAPS * K, nrows), F32),
        pltpu.VMEM((BAND, nrows), F32),
        pltpu.VMEM((nrows + 16, BAND), F32),
        pltpu.VMEM((BAND // 128, 2 * rows * K, 128), F32),
        pltpu.VMEM((ext, K, BAND), F32),
        pltpu.VMEM((ext, K, BAND), F32),
        pltpu.VMEM((2, C, C), F32),
        pltpu.VMEM((K, half, C), F32),
        pltpu.VMEM((K, half, C), BF16),
        pltpu.VMEM((K, half, C), BF16),
        pltpu.VMEM((2, K // 2, half // 4, C), BF16),
        pltpu.VMEM((2, K // 2, half // 4, C), BF16),
        pltpu.VMEM((2, K, half // 4, C), BF16),
        pltpu.VMEM((2, K, half // 4, C), BF16),
        pltpu.VMEM((K, half // 4, C), F32),
        pltpu.VMEM((3, 2, half // 4, C), BF16),
        pltpu.VMEM((3, 2, half // 4, C), BF16),
        pltpu.VMEM((2, half // 4, C), F32),
        pltpu.VMEM((3, half // 8, C), F32),
        dma((4,)),
        dma((2, 16)), dma((2, 12)),
        dma((2,)), dma((2,)),
        dma((2, 2)), dma((2, 2)),
        dma((2, 2)), dma((2, 2)),
        dma((3,)), dma((3,)),
        dma((3,)), dma((3,)),
    ]
    results = pl.pallas_call(
        kernel,
        out_shape=(
            jax.ShapeDtypeStruct((cols, rows, C), BF16),
            jax.ShapeDtypeStruct((cols, rows, C), BF16),
            jax.ShapeDtypeStruct((half // 8, C), F32),
        ),
        in_specs=[pl.BlockSpec(memory_space=pltpu.SMEM)] + [anywhere] * 4,
        out_specs=(vmem, vmem, vmem),
        scratch_shapes=scratch,
        compiler_params=pltpu.CompilerParams(
            collective_id=0, has_side_effects=True, vmem_limit_bytes=62 * 2**20),
    )(spans, cotangent.transpose(by_lon), inputs.transpose(by_lon),
      basis.transpose(2, 3, 1, 0), weight)
    output, grad_inputs, grad_weight = pl.pallas_call(
        hand_over,
        out_shape=[jax.ShapeDtypeStruct(r.shape, r.dtype) for r in results],
        in_specs=[anywhere] * 3,
        out_specs=[anywhere] * 3,
        scratch_shapes=[pltpu.VMEM(r.shape, r.dtype) for r in results] + [dma((7,)), dma((7,))],
    )(*results)
    return output.transpose(by_lon), grad_inputs.transpose(by_lon), grad_weight


def solution(mesh):
    in_specs = (P("lat", "lon", None), P(), P(), P(), P("lat", "lon", None))
    out_specs = (P("lat", "lon", None), P("lat", "lon", None), P(("lon", "lat"), None))
    return jax.shard_map(shards, mesh=mesh, in_specs=in_specs, out_specs=out_specs, check_vma=False)
```

```python
import functools
import math

import jax
import jax.numpy as jnp
from jax import lax
from jax.experimental import pallas as pl
from jax.experimental.pallas import tpu as pltpu
from jax.sharding import PartitionSpec as P

RR = 2
SMAX = 45
REACH = 2 * RR + 1
TAPS = 2 * SMAX + 1
B = 48
W = 144
LEAD = 3
BAND = 768
MESH = pl.DeviceIdType.MESH
F32 = jnp.float32
BF16 = jnp.bfloat16


def dot(a, b):
    return jnp.dot(a, b, preferred_element_type=F32)


def kernel(
    spans, cot_hbm, x_hbm, basis_hbm, weight_hbm,
    out_ref, gin_ref, gw_ref,
    wc, wx, own_c, own_x, sl_c, sl_x, rst_c, rst_x, relay_c, relay_x, flat, flat_out,
    bands, feat, weight, weight_t, xt, basis, basis_f, column, turned, near, taps, rtaps,
    tmp, gown, cs, cr, rs, rr, xs, xr, s2, ys, yr, s3, zr,
    load_sem, hs_send, hs_recv, cs_send, cs_recv, rs_send, rs_recv, xs_send, xs_recv,
    ys_send, ys_recv, zs_send, zs_recv,
):
    cols, rows, C = x_hbm.shape
    K = weight_hbm.shape[0] // C
    tiles = C // 128
    lon, lat = lax.axis_index("lon"), lax.axis_index("lat")
    nlon, nlat = lax.axis_size("lon"), lax.axis_size("lat")
    core, zl, y = lon % 2, (lon // 2) % 2, lon // 4
    x, zh = lat % 4, lat // 4
    right, left = lax.rem(lon + 1, nlon), lax.rem(lon + nlon - 1, nlon)
    not_first, not_last = lat > 0, lat < nlat - 1
    far_above = jnp.logical_and(not_first, x == 0)
    far_below = jnp.logical_and(not_last, x == 3)
    near_above = jnp.logical_and(not_first, x != 0)
    near_below = jnp.logical_and(not_last, x != 3)

    def at(lon_, lat_):
        return {"lon": lon_, "lat": lat_}

    def lon_of(y_, zl_, core_):
        return (y_ * 2 + zl_) * 2 + core_

    core_dev = at(lon_of(y, zl, 1 - core), lat)
    x_devs = [at(lon, zh * 4 + (x + d) % 4) for d in (1, 3)]
    y_devs = [at(lon_of((y + d) % 4, zl, core), lat) for d in (1, 2, 3)]
    z_steps = ((0, 1), (1, 0), (1, 1))
    z_devs = [
        at(lon_of(y, (zl + a) % 2, core), ((zh + b) % 2) * 4 + x) for a, b in z_steps
    ]

    loads = [
        pltpu.make_async_copy(cot_hbm, gin_ref, load_sem.at[0]),
        pltpu.make_async_copy(x_hbm, out_ref, load_sem.at[1]),
        pltpu.make_async_copy(basis_hbm, basis, load_sem.at[2]),
        pltpu.make_async_copy(weight_hbm, weight, load_sem.at[3]),
    ]
    loads[0].start()

    barrier = pltpu.get_barrier_semaphore()

    def greet(device):
        pl.semaphore_signal(barrier, inc=1, device_id=device, device_id_type=MESH)

    for device in [at(left, lat), at(right, lat), core_dev] + x_devs + y_devs + z_devs:
        greet(device)

    pl.when(not_first)(lambda: greet(at(lon, lat - 1)))
    pl.when(not_last)(lambda: greet(at(lon, lat + 1)))

    chunks = ((0, 8), (8, 4), (12, 4))

    def halo(t, own, sl, w, rst, relay):
        plan = []
        for start, n in chunks:
            plan.append((sl.at[pl.ds(start, n)],
                         w.at[pl.ds(RR + start, n), pl.ds(0, B), pl.ds(0, C)],
                         at(right, lat), None, None))
        for start, n in chunks:
            plan.append((own.at[pl.ds(start, n), pl.ds(0, B)],
                         rst.at[pl.ds(RR + start, n)], at(left, lat), None, None))
        low, high = pl.ds(0, RR), pl.ds(rows - RR, RR)
        above, below = pl.ds(0, RR), pl.ds(rows + RR, RR)
        for src, dst, step, here, there in (
            (high, above, 1, not_last, not_first), (low, below, -1, not_first, not_last)
        ):
            plan.append((own.at[src], w.at[dst, pl.ds(0, 2 * B), pl.ds(C, C)],
                         at(lon, lat + step), here, there))
        for n, dst, here, there in (
            (0, above, far_above, not_first), (1, below, far_below, not_last)
        ):
            plan.append((relay.at[n], w.at[dst, pl.ds(0, B), pl.ds(0, C)],
                         at(right, lat), here, there))
            plan.append((w.at[dst, pl.ds(0, B), pl.ds(C, C)], rst.at[dst],
                         at(left, lat), here, there))
        for src, dst, step, here in (
            (pl.ds(rows, RR), above, 1, near_below), (pl.ds(RR, RR), below, -1, near_above)
        ):
            side = (pl.ds(0, B), pl.ds(0, C))
            plan.append((w.at[(src,) + side], w.at[(dst,) + side],
                         at(lon, lat + step), here, None))
            plan.append((rst.at[src], rst.at[dst], at(lon, lat + step), here, None))
        return [
            (pltpu.make_async_remote_copy(
                src_ref=src, dst_ref=dst, send_sem=hs_send.at[t, i],
                recv_sem=hs_recv.at[t, i if i < 12 else i - 4], device_id=device, device_id_type=MESH),
             here, there)
            for i, (src, dst, device, here, there) in enumerate(plan)
        ]

    halo_c = halo(0, own_c, sl_c, wc, rst_c, relay_c)
    halo_x = halo(1, own_x, sl_x, wx, rst_x, relay_x)

    def guarded(condition, action):
        if condition is None:
            action()
        else:
            pl.when(condition)(action)

    def start(plan, indices):
        for i in indices:
            guarded(plan[i][1], plan[i][0].start)

    def arrive(plan, indices):
        for i in indices:
            guarded(plan[i][2], plan[i][0].wait_recv)

    def sent(plan, indices):
        for i in indices:
            guarded(plan[i][1], plan[i][0].wait_send)

    def widen(raw):
        def step(j, _):
            ten = pl.ds(pl.multiple_of(j * 10 * rows, 8), 10 * rows)
            block = raw[pl.ds(j * 10, 10)].reshape(10 * rows, C).astype(F32)
            for n in range(tiles):
                flat[n, ten] = block[:, n * 128:(n + 1) * 128]
            return 0
        lax.fori_loop(0, cols // 10, step, 0, unroll=3)

    def stage(first, n_rows, own, sl):
        def step(p, _):
            for n in range(tiles):
                at_n = pl.ds(n * 128, 128)
                own[p, 0:cols, at_n] = flat[n, pl.ds(p, cols, stride=rows)].astype(BF16)
                sl[p, :, at_n] = (
                    flat[n, pl.ds((cols - B) * rows + p, B, stride=rows)].astype(BF16))
            own[p, cols:2 * B] = jnp.zeros((2 * B - cols, C), BF16)
            return 0
        lax.fori_loop(first, first + n_rows, step, 0, unroll=2)

    def pass_on(plan, w, relay):
        def one(n, first):
            plan[6 + n][0].wait_recv()
            relay[n] = w[first:first + RR, cols - B:cols, C:2 * C]
            for i in (8 + 2 * n, 9 + 2 * n):
                plan[i][0].start()
        pl.when(far_above)(lambda: one(0, 0))
        pl.when(far_below)(lambda: one(1, rows + RR))

    def place(own, w):
        def step(p, _):
            w[p + RR, B:B + cols, 0:C] = own[p, 0:cols]
            w[p + RR, 0:2 * B, C:2 * C] = own[p]
            return 0
        lax.fori_loop(0, rows, step, 0, unroll=2)

        def pad(p, _):
            w[p, B + cols:W, C:2 * C] = jnp.zeros((W - B - cols, C), BF16)
            return 0
        lax.fori_loop(0, rows + 2 * RR, pad, 0)

        def clear(first):
            for p in range(RR):
                w[first + p] = jnp.zeros((W, 2 * C), BF16)

        pl.when(lat == 0)(lambda: clear(0))
        pl.when(lat == nlat - 1)(lambda: clear(rows + RR))

    def right_edge(first, n, w, rst):
        def step(j, _):
            p = first + j
            r = rst[p]
            w[p, cols:cols + B, C:2 * C] = r
            w[p, B + cols:W, 0:C] = r[0:W - B - cols]
            return 0
        lax.fori_loop(0, n, step, 0, unroll=2)

    def outer_rows(first, w, rst):
        for p in range(RR):
            w[first + p, B:B + cols, 0:C] = w[first + p, 0:cols, C:2 * C]
        right_edge(first, RR, w, rst)

    def build_band(row_taps, i):
        for k in range(K):
            v = jnp.broadcast_to(row_taps[k:k + 1], (B, BAND))
            v = pltpu.roll(v, 0, 1, stride=1, stride_axis=0)
            bands[i, k * B:(k + 1) * B] = v.astype(BF16)

    def convolve(plan, w, rst, needs, before):
        def group(g, _):
            for n in range(len(chunks)):
                @pl.when(g == n)
                def _():
                    before(n)
                    for c in needs[n]:
                        arrive(plan, (c, 3 + c))
                        right_edge(RR + chunks[c][0], chunks[c][1], w, rst)
                        if c == 0:
                            start(plan, (14, 15))
                        if c == 2:
                            start(plan, (12, 13))

            @pl.when(g == len(chunks))
            def _():
                before(len(chunks))
                pl.when(near_above)(plan[6][0].wait_recv)
                pl.when(near_below)(plan[7][0].wait_recv)
                arrive(plan, (8, 9, 10, 11))
                pl.when(not_first)(lambda: outer_rows(0, w, rst))
                pl.when(not_last)(lambda: outer_rows(rows + RR, w, rst))

            for u in range(4):
                outer = u if u < RR else rows - 4 + u
                i = jnp.where(g < len(chunks), RR + 4 * g + u, outer)
                window = w[pl.ds(i, REACH)].reshape(REACH * W, 2 * C)
                acc = dot(bands[i, :, 0:REACH * W], window).astype(BF16)
                for k in range(K):
                    for b in range(2):
                        place_at = pl.ds(pl.multiple_of(i * 2 * B + b * B, 16), B)
                        feat[place_at, k * C:(k + 1) * C] = (
                            acc[k * B:(k + 1) * B, b * C:(b + 1) * C])
            return 0
        lax.fori_loop(0, len(chunks) + 1, group, 0)

    loads[0].wait()
    for load in (loads[2], loads[1], loads[3]):
        load.start()
    widen(gin_ref)
    stage(0, 8, own_c, sl_c)
    pl.semaphore_wait(
        barrier, 11 + jnp.where(not_first, 1, 0) + jnp.where(not_last, 1, 0))
    start(halo_c, (0, 3, 7))
    stage(8, 8, own_c, sl_c)
    start(halo_c, (6,))
    place(own_c, wc)

    loads[2].wait()
    basis_f[...] = basis[...].astype(F32).reshape(basis_f.shape)
    column[...] = jnp.zeros(column.shape, F32)
    turned[...] = jnp.zeros(turned.shape, F32)
    first_row = lat * rows
    for k in range(K):
        for a in range(REACH):
            column[a * W + LEAD:a * W + LEAD + TAPS] = (
                basis_f[pl.ds(a * TAPS * K + k, TAPS, stride=K)])
        turned[8:8 + nlat * rows] = column[...].T
        for n in range(BAND // 128):
            near[n, pl.ds(k, 2 * rows, stride=K)] = turned[
                pl.ds(pl.multiple_of(first_row, 8), 2 * rows), n * 128:(n + 1) * 128]
    lane = lax.broadcasted_iota(jnp.int32, (K, BAND), 1)
    away = jnp.abs(lax.rem(lane, W) - LEAD - SMAX)

    def mask_row(e, _):
        row = jnp.clip(first_row + e - RR, 0, nlat * rows - 1)
        at_e = pl.ds(pl.multiple_of((e + 8 - RR) * K, 8), K)
        v = jnp.concatenate([near[n, at_e] for n in range(BAND // 128)], axis=1)
        taps[e] = jnp.where(away <= spans[row], v, 0.0)
        return 0
    lax.fori_loop(0, rows + 2 * RR, mask_row, 0, unroll=4)

    flip = (lax.broadcasted_iota(jnp.int32, (128, 128), 0)
            + lax.broadcasted_iota(jnp.int32, (128, 128), 1))
    flip = jnp.where(flip == 127, 1.0, 0.0).astype(BF16)
    every = taps[...].reshape((rows + 2 * RR) * K, BAND).astype(BF16)
    last = BAND // 128 - 1
    every = jnp.concatenate(
        [dot(every[:, (last - n) * 128:(last - n + 1) * 128], flip)
         for n in range(last + 1)], axis=1)
    every = pltpu.roll(every, (REACH - 1) * W + 2 * B + 1, 1)
    rtaps[...] = every.reshape(rows + 2 * RR, K, BAND)

    def reverse_band(i, _):
        v = rtaps[i]
        for a in range(1, REACH):
            v = jnp.where(lane >= a * W, rtaps[i + a], v)
        build_band(v, i)
        return 0
    lax.fori_loop(0, rows // 2, reverse_band, 0, unroll=2)
    start(halo_c, (1, 4))
    lax.fori_loop(rows // 2, rows, reverse_band, 0, unroll=2)
    start(halo_c, (2, 5))

    def turn(k, _):
        at_k = pl.ds(pl.multiple_of(k * C, C), C)
        weight_t[at_k] = weight[at_k].T
        return 0

    def while_adjoint(n):
        if n == 0:
            pass_on(halo_c, wc, relay_c)
        elif n == 1:
            loads[1].wait()
            widen(out_ref)
            stage(0, 8, own_x, sl_x)
        elif n == 2:
            stage(8, 8, own_x, sl_x)
            place(own_x, wx)
            for g in range(4):
                xt[:, g * C:(g + 1) * C] = own_x[4 * g:4 * g + 4].reshape(C, C).T
        elif n == 3:
            start(halo_x, (6, 7, 0, 3))
            loads[3].wait()
            lax.fori_loop(0, K, turn, 0, unroll=2)

    convolve(halo_c, wc, rst_c, ((0,), (1,), (2,)), while_adjoint)
    start(halo_x, (1, 4, 2, 5))

    part = K // 2

    def core_copy(j):
        these = pl.ds(part * j, part)
        return pltpu.make_async_remote_copy(
            src_ref=cs.at[these], dst_ref=cr.at[these], send_sem=cs_send.at[j],
            recv_sem=cs_recv.at[j], device_id=core_dev, device_id_type=MESH)

    def relay_copy(j, h):
        these = pl.ds(part // 2 * j, part // 2)
        return pltpu.make_async_remote_copy(
            src_ref=rs.at[h, these], dst_ref=rr.at[h, these], send_sem=rs_send.at[j, h],
            recv_sem=rs_recv.at[j, h], device_id=x_devs[h], device_id_type=MESH)

    def x_copy(d, j):
        these = pl.ds(part * j, part)
        return pltpu.make_async_remote_copy(
            src_ref=xs.at[d, these], dst_ref=xr.at[d, these], send_sem=xs_send.at[d, j],
            recv_sem=xs_recv.at[d, j], device_id=x_devs[d], device_id_type=MESH)

    def quarter(k, x_):
        return jnp.concatenate(
            [gown[k, pl.ds(pl.multiple_of(x_ * 24, 8), 24)],
             gown[k, pl.ds(pl.multiple_of(96 + x_ * 24, 8), 24)]], axis=0)

    def opposite_stage(j):
        core_copy(j).wait_recv()
        for k in range(part * j, part * (j + 1)):
            gown[k] = gown[k] + cr[k].astype(F32)
            rs[k % 2, k // 2] = quarter(k, (x + 2) % 4).astype(BF16)
        for h in range(2):
            relay_copy(j, h).start()

    def x_stage(j):
        for h in range(2):
            relay_copy(j, h).wait_recv()
        for k in range(part * j, part * (j + 1)):
            for d, step in enumerate((1, 3)):
                share = quarter(k, (x + step) % 4)
                if d == k % 2:
                    share = share + rr[k % 2, k // 2].astype(F32)
                xs[d, k] = share.astype(BF16)
        for d in range(2):
            x_copy(d, j).start()

    half = C // 2

    def grad_pair(j, _):
        acc = dot(xt[...], feat[:, pl.ds(pl.multiple_of(j * 2 * C, 2 * C), 2 * C)])
        for u in range(4):
            build_band(taps[RR + 4 * j + u], 4 * j + u)
        for h in range(2):
            tmp[h] = acc[:, h * C:(h + 1) * C]
        for h in range(2):
            k = 2 * j + h
            gown[k] = tmp[h, pl.ds(pl.multiple_of(core * half, half), half)]
            cs[k] = tmp[h, pl.ds(pl.multiple_of((1 - core) * half, half), half)].astype(BF16)
        pl.when(j == 1)(lambda: core_copy(0).start())

        @pl.when(j == 3)
        def _():
            core_copy(1).start()
            opposite_stage(0)
        return 0
    lax.fori_loop(0, K // 2, grad_pair, 0)

    per = rows // 2
    m = per * 2 * B

    def mix(j, matrix):
        return dot(feat[j * m:(j + 1) * m], matrix[...])

    sent(halo_c, (3, 4, 5, 6, 7))
    for j in range(2):
        acc = mix(j, weight_t).astype(BF16)
        for i in range(per):
            own_c[j * per + i] = acc[i * 2 * B:(i + 1) * 2 * B]
        if j == 0:
            opposite_stage(1)
            x_stage(0)
            pass_on(halo_x, wx, relay_x)
    x_stage(1)


    def y_copy(d):
        return pltpu.make_async_remote_copy(
            src_ref=ys.at[d], dst_ref=yr.at[d], send_sem=ys_send.at[d],
            recv_sem=ys_recv.at[d], device_id=y_devs[d], device_id_type=MESH)

    def add_x(k, _):
        s2[k] = quarter(k, x) + xr[0, k].astype(F32) + xr[1, k].astype(F32)
        return 0

    def y_stage():
        for j in range(2):
            for d in range(2):
                x_copy(d, j).wait_recv()
        lax.fori_loop(0, K, add_x, 0)
        for d in range(3):
            ys[d] = s2[pl.ds(((y + d + 1) % 4) * 2, 2)].astype(BF16)
            y_copy(d).start()

    def while_forward(n):
        if n == 3:
            y_stage()

    convolve(halo_x, wx, rst_x, ((0, 1, 2), (), ()), while_forward)

    def z_copy(d):
        a, b = z_steps[d]
        src = s3.at[(zl + a) % 2, pl.ds(pl.multiple_of(((zh + b) % 2) * 24, 8), 24)]
        return pltpu.make_async_remote_copy(
            src_ref=src, dst_ref=zr.at[d], send_sem=zs_send.at[d],
            recv_sem=zs_recv.at[d], device_id=z_devs[d], device_id_type=MESH)

    def z_stage():
        for d in range(3):
            y_copy(d).wait_recv()
        s3[...] = s2[pl.ds(y * 2, 2)] + sum(yr[d].astype(F32) for d in range(3))
        for d in range(3):
            z_copy(d).start()

    def narrow(wide, result):
        def step(j, _):
            ten = pl.ds(pl.multiple_of(j * 10 * rows, 8), 10 * rows)
            block = jnp.concatenate([wide[n, ten] for n in range(tiles)], axis=1)
            result[pl.ds(j * 10, 10)] = block.astype(BF16).reshape(10, rows, C)
            return 0
        lax.fori_loop(0, cols // 10, step, 0, unroll=True)

    for j in range(2):
        if j == 0:
            for p in range(rows):
                for n in range(tiles):
                    flat[n, pl.ds(p, cols, stride=rows)] = (
                        own_c[p, 0:cols, n * 128:(n + 1) * 128].astype(F32))
        else:
            z_stage()
            narrow(flat, gin_ref)
        acc = mix(j, weight)
        for i in range(per):
            for n in range(tiles):
                flat_out[n, pl.ds(j * per + i, cols, stride=rows)] = (
                    acc[i * 2 * B:i * 2 * B + cols, n * 128:(n + 1) * 128])
    narrow(flat_out, out_ref)

    for d in range(3):
        z_copy(d).wait_recv()
    total = s3[zl, pl.ds(pl.multiple_of(zh * 24, 8), 24)] + sum(zr[d] for d in range(3))
    scale = 1.0 / math.sqrt(rows * nlat * cols * nlon)
    gw_ref[...] = total * scale

    for plan in (halo_c, halo_x):
        sent(plan, (0, 1, 2, 8, 9, 10, 11, 12, 13, 14, 15) + ((3, 4, 5, 6, 7) if plan is halo_x else ()))
    for j in range(2):
        core_copy(j).wait_send()
        for d in range(2):
            relay_copy(j, d).wait_send()
            x_copy(d, j).wait_send()
    for d in range(3):
        y_copy(d).wait_send()
        z_copy(d).wait_send()


def hand_over(out, gin, gw, out_to, gin_to, gw_to, out_v, gin_v, gw_v, sem_in, sem_out):
    parts = 3
    n = out.shape[0] // parts
    moves = []
    for i in range(parts):
        piece = pl.ds(i * n, n)
        moves.append((out.at[piece], out_v.at[piece], out_to.at[piece]))
        moves.append((gin.at[piece], gin_v.at[piece], gin_to.at[piece]))
    moves.append((gw, gw_v, gw_to))
    arriving = [
        pltpu.make_async_copy(a, b, sem_in.at[i]) for i, (a, b, _) in enumerate(moves)]
    leaving = [
        pltpu.make_async_copy(b, c, sem_out.at[i]) for i, (_, b, c) in enumerate(moves)]
    for copy in arriving:
        copy.start()
    for first, second in zip(arriving, leaving):
        first.wait()
        second.start()
    for copy in leaving:
        copy.wait()


def shards(inputs, basis, spans, weight, cotangent):
    rows, cols, C = inputs.shape
    K = weight.shape[0] // C
    nrows = basis.shape[0]
    by_lon = (1, 0, 2)
    ext = rows + 2 * RR
    vmem = pl.BlockSpec(memory_space=pltpu.VMEM)
    anywhere = pl.BlockSpec(memory_space=pl.ANY)
    own_cols = 2 * B
    dma = pltpu.SemaphoreType.DMA
    half = C // 2
    scratch = [
        pltpu.VMEM((ext, W, 2 * C), BF16),
        pltpu.VMEM((ext, W, 2 * C), BF16),
        pltpu.VMEM((rows, own_cols, C), BF16),
        pltpu.VMEM((rows, own_cols, C), BF16),
        pltpu.VMEM((rows, B, C), BF16),
        pltpu.VMEM((rows, B, C), BF16),
        pltpu.VMEM((ext, B, C), BF16),
        pltpu.VMEM((ext, B, C), BF16),
        pltpu.VMEM((2, RR, B, C), BF16),
        pltpu.VMEM((2, RR, B, C), BF16),
        pltpu.VMEM((C // 128, cols * rows, 128), F32),
        pltpu.VMEM((C // 128, cols * rows, 128), F32),
        pltpu.VMEM((rows, K * B, BAND), BF16),
        pltpu.VMEM((rows * own_cols, K * C), BF16),
        pltpu.VMEM((K * C, C), BF16),
        pltpu.VMEM((K * C, C), BF16),
        pltpu.VMEM((C, rows * own_cols), BF16),
        pltpu.VMEM((REACH, TAPS, K, nrows), BF16),
        pltpu.VMEM((REACH * TAPS * K, nrows), F32),
        pltpu.VMEM((BAND, nrows), F32),
        pltpu.VMEM((nrows + 16, BAND), F32),
        pltpu.VMEM((BAND // 128, 2 * rows * K, 128), F32),
        pltpu.VMEM((ext, K, BAND), F32),
        pltpu.VMEM((ext, K, BAND), F32),
        pltpu.VMEM((2, C, C), F32),
        pltpu.VMEM((K, half, C), F32),
        pltpu.VMEM((K, half, C), BF16),
        pltpu.VMEM((K, half, C), BF16),
        pltpu.VMEM((2, K // 2, half // 4, C), BF16),
        pltpu.VMEM((2, K // 2, half // 4, C), BF16),
        pltpu.VMEM((2, K, half // 4, C), BF16),
        pltpu.VMEM((2, K, half // 4, C), BF16),
        pltpu.VMEM((K, half // 4, C), F32),
        pltpu.VMEM((3, 2, half // 4, C), BF16),
        pltpu.VMEM((3, 2, half // 4, C), BF16),
        pltpu.VMEM((2, half // 4, C), F32),
        pltpu.VMEM((3, half // 8, C), F32),
        dma((4,)),
        dma((2, 16)), dma((2, 12)),
        dma((2,)), dma((2,)),
        dma((2, 2)), dma((2, 2)),
        dma((2, 2)), dma((2, 2)),
        dma((3,)), dma((3,)),
        dma((3,)), dma((3,)),
    ]
    results = pl.pallas_call(
        kernel,
        out_shape=(
            jax.ShapeDtypeStruct((cols, rows, C), BF16),
            jax.ShapeDtypeStruct((cols, rows, C), BF16),
            jax.ShapeDtypeStruct((half // 8, C), F32),
        ),
        in_specs=[pl.BlockSpec(memory_space=pltpu.SMEM)] + [anywhere] * 4,
        out_specs=(vmem, vmem, vmem),
        scratch_shapes=scratch,
        compiler_params=pltpu.CompilerParams(
            collective_id=0, has_side_effects=True, vmem_limit_bytes=62 * 2**20),
    )(spans, cotangent.transpose(by_lon), inputs.transpose(by_lon),
      basis.transpose(2, 3, 1, 0), weight)
    output, grad_inputs, grad_weight = pl.pallas_call(
        hand_over,
        out_shape=[jax.ShapeDtypeStruct(r.shape, r.dtype) for r in results],
        in_specs=[anywhere] * 3,
        out_specs=[anywhere] * 3,
        scratch_shapes=[pltpu.VMEM(r.shape, r.dtype) for r in results] + [dma((7,)), dma((7,))],
    )(*results)
    return output.transpose(by_lon), grad_inputs.transpose(by_lon), grad_weight


def solution(mesh):
    in_specs = (P("lat", "lon", None), P(), P(), P(), P("lat", "lon", None))
    out_specs = (P("lat", "lon", None), P("lat", "lon", None), P(("lon", "lat"), None))
    return jax.shard_map(shards, mesh=mesh, in_specs=in_specs, out_specs=out_specs, check_vma=False)
```

```python
import functools
import math

import jax
import jax.numpy as jnp
from jax import lax
from jax.experimental import pallas as pl
from jax.experimental.pallas import tpu as pltpu
from jax.sharding import PartitionSpec as P

RR = 2
SMAX = 45
REACH = 2 * RR + 1
TAPS = 2 * SMAX + 1
B = 48
W = 144
LEAD = 3
BAND = 768
MESH = pl.DeviceIdType.MESH
F32 = jnp.float32
BF16 = jnp.bfloat16


def dot(a, b):
    return jnp.dot(a, b, preferred_element_type=F32)


def kernel(
    spans, cot_hbm, x_hbm, basis_hbm, weight_hbm,
    out_hbm, gin_hbm, gw_ref,
    out_ref, gin_ref,
    wc, wx, own_c, own_x, sl_c, sl_x, rst_c, rst_x, relay_c, relay_x, flat, flat_out,
    bands, feat, weight, weight_t, xt, basis, basis_f, column, turned, near, taps, rtaps,
    tmp, gown, cs, cr, rs, rr, xs, xr, s2, ys, yr, s3, zr,
    load_sem, store_sem, hs_send, hs_recv, cs_send, cs_recv, rs_send, rs_recv, xs_send, xs_recv,
    ys_send, ys_recv, zs_send, zs_recv,
):
    cols, rows, C = x_hbm.shape
    K = weight_hbm.shape[0] // C
    tiles = C // 128
    lon, lat = lax.axis_index("lon"), lax.axis_index("lat")
    nlon, nlat = lax.axis_size("lon"), lax.axis_size("lat")
    core, zl, y = lon % 2, (lon // 2) % 2, lon // 4
    x, zh = lat % 4, lat // 4
    right, left = lax.rem(lon + 1, nlon), lax.rem(lon + nlon - 1, nlon)
    not_first, not_last = lat > 0, lat < nlat - 1
    far_above = jnp.logical_and(not_first, x == 0)
    far_below = jnp.logical_and(not_last, x == 3)
    near_above = jnp.logical_and(not_first, x != 0)
    near_below = jnp.logical_and(not_last, x != 3)

    def at(lon_, lat_):
        return {"lon": lon_, "lat": lat_}

    def lon_of(y_, zl_, core_):
        return (y_ * 2 + zl_) * 2 + core_

    core_dev = at(lon_of(y, zl, 1 - core), lat)
    x_devs = [at(lon, zh * 4 + (x + d) % 4) for d in (1, 3)]
    y_devs = [at(lon_of((y + d) % 4, zl, core), lat) for d in (1, 2, 3)]
    z_steps = ((0, 1), (1, 0), (1, 1))
    z_devs = [
        at(lon_of(y, (zl + a) % 2, core), ((zh + b) % 2) * 4 + x) for a, b in z_steps
    ]

    loads = [
        pltpu.make_async_copy(cot_hbm, gin_ref, load_sem.at[0]),
        pltpu.make_async_copy(x_hbm, out_ref, load_sem.at[1]),
        pltpu.make_async_copy(basis_hbm, basis, load_sem.at[2]),
        pltpu.make_async_copy(weight_hbm, weight, load_sem.at[3]),
    ]
    loads[0].start()

    barrier = pltpu.get_barrier_semaphore()

    def greet(device):
        pl.semaphore_signal(barrier, inc=1, device_id=device, device_id_type=MESH)

    for device in [at(left, lat), at(right, lat), core_dev] + x_devs + y_devs + z_devs:
        greet(device)

    pl.when(not_first)(lambda: greet(at(lon, lat - 1)))
    pl.when(not_last)(lambda: greet(at(lon, lat + 1)))

    chunks = ((0, 8), (8, 4), (12, 4))

    def halo(t, own, sl, w, rst, relay):
        plan = []
        for start, n in chunks:
            plan.append((sl.at[pl.ds(start, n)],
                         w.at[pl.ds(RR + start, n), pl.ds(0, B), pl.ds(0, C)],
                         at(right, lat), None, None))
        for start, n in chunks:
            plan.append((own.at[pl.ds(start, n), pl.ds(0, B)],
                         rst.at[pl.ds(RR + start, n)], at(left, lat), None, None))
        low, high = pl.ds(0, RR), pl.ds(rows - RR, RR)
        above, below = pl.ds(0, RR), pl.ds(rows + RR, RR)
        for src, dst, step, here, there in (
            (high, above, 1, not_last, not_first), (low, below, -1, not_first, not_last)
        ):
            plan.append((own.at[src], w.at[dst, pl.ds(0, 2 * B), pl.ds(C, C)],
                         at(lon, lat + step), here, there))
        for n, dst, here, there in (
            (0, above, far_above, not_first), (1, below, far_below, not_last)
        ):
            plan.append((relay.at[n], w.at[dst, pl.ds(0, B), pl.ds(0, C)],
                         at(right, lat), here, there))
            plan.append((w.at[dst, pl.ds(0, B), pl.ds(C, C)], rst.at[dst],
                         at(left, lat), here, there))
        for src, dst, step, here in (
            (pl.ds(rows, RR), above, 1, near_below), (pl.ds(RR, RR), below, -1, near_above)
        ):
            side = (pl.ds(0, B), pl.ds(0, C))
            plan.append((w.at[(src,) + side], w.at[(dst,) + side],
                         at(lon, lat + step), here, None))
            plan.append((rst.at[src], rst.at[dst], at(lon, lat + step), here, None))
        return [
            (pltpu.make_async_remote_copy(
                src_ref=src, dst_ref=dst, send_sem=hs_send.at[t, i],
                recv_sem=hs_recv.at[t, i if i < 12 else i - 4], device_id=device, device_id_type=MESH),
             here, there)
            for i, (src, dst, device, here, there) in enumerate(plan)
        ]

    halo_c = halo(0, own_c, sl_c, wc, rst_c, relay_c)
    halo_x = halo(1, own_x, sl_x, wx, rst_x, relay_x)

    def guarded(condition, action):
        if condition is None:
            action()
        else:
            pl.when(condition)(action)

    def start(plan, indices):
        for i in indices:
            guarded(plan[i][1], plan[i][0].start)

    def arrive(plan, indices):
        for i in indices:
            guarded(plan[i][2], plan[i][0].wait_recv)

    def sent(plan, indices):
        for i in indices:
            guarded(plan[i][1], plan[i][0].wait_send)

    def widen(raw):
        def step(j, _):
            ten = pl.ds(pl.multiple_of(j * 10 * rows, 8), 10 * rows)
            block = raw[pl.ds(j * 10, 10)].reshape(10 * rows, C).astype(F32)
            for n in range(tiles):
                flat[n, ten] = block[:, n * 128:(n + 1) * 128]
            return 0
        lax.fori_loop(0, cols // 10, step, 0, unroll=3)

    def stage(first, n_rows, own, sl):
        def step(p, _):
            for n in range(tiles):
                at_n = pl.ds(n * 128, 128)
                own[p, 0:cols, at_n] = flat[n, pl.ds(p, cols, stride=rows)].astype(BF16)
                sl[p, :, at_n] = (
                    flat[n, pl.ds((cols - B) * rows + p, B, stride=rows)].astype(BF16))
            own[p, cols:2 * B] = jnp.zeros((2 * B - cols, C), BF16)
            return 0
        lax.fori_loop(first, first + n_rows, step, 0, unroll=2)

    def pass_on(plan, w, relay):
        def one(n, first):
            plan[6 + n][0].wait_recv()
            relay[n] = w[first:first + RR, cols - B:cols, C:2 * C]
            for i in (8 + 2 * n, 9 + 2 * n):
                plan[i][0].start()
        pl.when(far_above)(lambda: one(0, 0))
        pl.when(far_below)(lambda: one(1, rows + RR))

    def place(own, w):
        def step(p, _):
            w[p + RR, B:B + cols, 0:C] = own[p, 0:cols]
            w[p + RR, 0:2 * B, C:2 * C] = own[p]
            return 0
        lax.fori_loop(0, rows, step, 0, unroll=2)

        def pad(p, _):
            w[p, B + cols:W, C:2 * C] = jnp.zeros((W - B - cols, C), BF16)
            return 0
        lax.fori_loop(0, rows + 2 * RR, pad, 0)

        def clear(first):
            for p in range(RR):
                w[first + p] = jnp.zeros((W, 2 * C), BF16)

        pl.when(lat == 0)(lambda: clear(0))
        pl.when(lat == nlat - 1)(lambda: clear(rows + RR))

    def right_edge(first, n, w, rst):
        def step(j, _):
            p = first + j
            r = rst[p]
            w[p, cols:cols + B, C:2 * C] = r
            w[p, B + cols:W, 0:C] = r[0:W - B - cols]
            return 0
        lax.fori_loop(0, n, step, 0, unroll=2)

    def outer_rows(first, w, rst):
        for p in range(RR):
            w[first + p, B:B + cols, 0:C] = w[first + p, 0:cols, C:2 * C]
        right_edge(first, RR, w, rst)

    def build_band(row_taps, i):
        for k in range(K):
            v = jnp.broadcast_to(row_taps[k:k + 1], (B, BAND))
            v = pltpu.roll(v, 0, 1, stride=1, stride_axis=0)
            bands[i, k * B:(k + 1) * B] = v.astype(BF16)

    def convolve(plan, w, rst, needs, before):
        def group(g, _):
            for n in range(len(chunks)):
                @pl.when(g == n)
                def _():
                    before(n)
                    for c in needs[n]:
                        arrive(plan, (c, 3 + c))
                        right_edge(RR + chunks[c][0], chunks[c][1], w, rst)
                        if c == 0:
                            start(plan, (14, 15))
                        if c == 2:
                            start(plan, (12, 13))

            @pl.when(g == len(chunks))
            def _():
                before(len(chunks))
                pl.when(near_above)(plan[6][0].wait_recv)
                pl.when(near_below)(plan[7][0].wait_recv)
                arrive(plan, (8, 9, 10, 11))
                pl.when(not_first)(lambda: outer_rows(0, w, rst))
                pl.when(not_last)(lambda: outer_rows(rows + RR, w, rst))

            for u in range(4):
                outer = u if u < RR else rows - 4 + u
                i = jnp.where(g < len(chunks), RR + 4 * g + u, outer)
                window = w[pl.ds(i, REACH)].reshape(REACH * W, 2 * C)
                acc = dot(bands[i, :, 0:REACH * W], window).astype(BF16)
                for k in range(K):
                    for b in range(2):
                        place_at = pl.ds(pl.multiple_of(i * 2 * B + b * B, 16), B)
                        feat[place_at, k * C:(k + 1) * C] = (
                            acc[k * B:(k + 1) * B, b * C:(b + 1) * C])
            return 0
        lax.fori_loop(0, len(chunks) + 1, group, 0)

    loads[0].wait()
    for load in (loads[2], loads[1], loads[3]):
        load.start()
    widen(gin_ref)
    stage(0, 8, own_c, sl_c)
    pl.semaphore_wait(
        barrier, 11 + jnp.where(not_first, 1, 0) + jnp.where(not_last, 1, 0))
    start(halo_c, (0, 3, 7))
    stage(8, 8, own_c, sl_c)
    start(halo_c, (6,))
    place(own_c, wc)

    loads[2].wait()
    basis_f[...] = basis[...].astype(F32).reshape(basis_f.shape)
    column[...] = jnp.zeros(column.shape, F32)
    turned[...] = jnp.zeros(turned.shape, F32)
    first_row = lat * rows
    for k in range(K):
        for a in range(REACH):
            column[a * W + LEAD:a * W + LEAD + TAPS] = (
                basis_f[pl.ds(a * TAPS * K + k, TAPS, stride=K)])
        turned[8:8 + nlat * rows] = column[...].T
        for n in range(BAND // 128):
            near[n, pl.ds(k, 2 * rows, stride=K)] = turned[
                pl.ds(pl.multiple_of(first_row, 8), 2 * rows), n * 128:(n + 1) * 128]
    lane = lax.broadcasted_iota(jnp.int32, (K, BAND), 1)
    away = jnp.abs(lax.rem(lane, W) - LEAD - SMAX)

    def mask_row(e, _):
        row = jnp.clip(first_row + e - RR, 0, nlat * rows - 1)
        at_e = pl.ds(pl.multiple_of((e + 8 - RR) * K, 8), K)
        v = jnp.concatenate([near[n, at_e] for n in range(BAND // 128)], axis=1)
        taps[e] = jnp.where(away <= spans[row], v, 0.0)
        return 0
    lax.fori_loop(0, rows + 2 * RR, mask_row, 0, unroll=4)

    flip = (lax.broadcasted_iota(jnp.int32, (128, 128), 0)
            + lax.broadcasted_iota(jnp.int32, (128, 128), 1))
    flip = jnp.where(flip == 127, 1.0, 0.0).astype(BF16)
    every = taps[...].reshape((rows + 2 * RR) * K, BAND).astype(BF16)
    last = BAND // 128 - 1
    every = jnp.concatenate(
        [dot(every[:, (last - n) * 128:(last - n + 1) * 128], flip)
         for n in range(last + 1)], axis=1)
    every = pltpu.roll(every, (REACH - 1) * W + 2 * B + 1, 1)
    rtaps[...] = every.reshape(rows + 2 * RR, K, BAND)

    def reverse_band(i, _):
        v = rtaps[i]
        for a in range(1, REACH):
            v = jnp.where(lane >= a * W, rtaps[i + a], v)
        build_band(v, i)
        return 0
    lax.fori_loop(0, rows // 2, reverse_band, 0, unroll=2)
    start(halo_c, (1, 4))
    lax.fori_loop(rows // 2, rows, reverse_band, 0, unroll=2)
    start(halo_c, (2, 5))

    def turn(k, _):
        at_k = pl.ds(pl.multiple_of(k * C, C), C)
        weight_t[at_k] = weight[at_k].T
        return 0

    def while_adjoint(n):
        if n == 0:
            pass_on(halo_c, wc, relay_c)
        elif n == 1:
            loads[1].wait()
            widen(out_ref)
            stage(0, 8, own_x, sl_x)
        elif n == 2:
            stage(8, 8, own_x, sl_x)
            place(own_x, wx)
            for g in range(4):
                xt[:, g * C:(g + 1) * C] = own_x[4 * g:4 * g + 4].reshape(C, C).T
        elif n == 3:
            start(halo_x, (6, 7, 0, 3))
            loads[3].wait()
            lax.fori_loop(0, K, turn, 0, unroll=2)

    convolve(halo_c, wc, rst_c, ((0,), (1,), (2,)), while_adjoint)
    start(halo_x, (1, 4, 2, 5))

    part = K // 2

    def core_copy(j):
        these = pl.ds(part * j, part)
        return pltpu.make_async_remote_copy(
            src_ref=cs.at[these], dst_ref=cr.at[these], send_sem=cs_send.at[j],
            recv_sem=cs_recv.at[j], device_id=core_dev, device_id_type=MESH)

    def relay_copy(j, h):
        these = pl.ds(part // 2 * j, part // 2)
        return pltpu.make_async_remote_copy(
            src_ref=rs.at[h, these], dst_ref=rr.at[h, these], send_sem=rs_send.at[j, h],
            recv_sem=rs_recv.at[j, h], device_id=x_devs[h], device_id_type=MESH)

    def x_copy(d, j):
        these = pl.ds(part * j, part)
        return pltpu.make_async_remote_copy(
            src_ref=xs.at[d, these], dst_ref=xr.at[d, these], send_sem=xs_send.at[d, j],
            recv_sem=xs_recv.at[d, j], device_id=x_devs[d], device_id_type=MESH)

    def quarter(k, x_):
        return jnp.concatenate(
            [gown[k, pl.ds(pl.multiple_of(x_ * 24, 8), 24)],
             gown[k, pl.ds(pl.multiple_of(96 + x_ * 24, 8), 24)]], axis=0)

    def opposite_stage(j):
        core_copy(j).wait_recv()
        for k in range(part * j, part * (j + 1)):
            gown[k] = gown[k] + cr[k].astype(F32)
            rs[k % 2, k // 2] = quarter(k, (x + 2) % 4).astype(BF16)
        for h in range(2):
            relay_copy(j, h).start()

    def x_stage(j):
        for h in range(2):
            relay_copy(j, h).wait_recv()
        for k in range(part * j, part * (j + 1)):
            for d, step in enumerate((1, 3)):
                share = quarter(k, (x + step) % 4)
                if d == k % 2:
                    share = share + rr[k % 2, k // 2].astype(F32)
                xs[d, k] = share.astype(BF16)
        for d in range(2):
            x_copy(d, j).start()

    half = C // 2

    def grad_pair(j, _):
        acc = dot(xt[...], feat[:, pl.ds(pl.multiple_of(j * 2 * C, 2 * C), 2 * C)])
        for u in range(4):
            build_band(taps[RR + 4 * j + u], 4 * j + u)
        for h in range(2):
            tmp[h] = acc[:, h * C:(h + 1) * C]
        for h in range(2):
            k = 2 * j + h
            gown[k] = tmp[h, pl.ds(pl.multiple_of(core * half, half), half)]
            cs[k] = tmp[h, pl.ds(pl.multiple_of((1 - core) * half, half), half)].astype(BF16)
        pl.when(j == 1)(lambda: core_copy(0).start())

        @pl.when(j == 3)
        def _():
            core_copy(1).start()
            opposite_stage(0)
        return 0
    lax.fori_loop(0, K // 2, grad_pair, 0)

    per = rows // 2
    m = per * 2 * B

    def mix(j, matrix):
        return dot(feat[j * m:(j + 1) * m], matrix[...])

    sent(halo_c, (3, 4, 5, 6, 7))
    for j in range(2):
        acc = mix(j, weight_t).astype(BF16)
        for i in range(per):
            own_c[j * per + i] = acc[i * 2 * B:(i + 1) * 2 * B]
        if j == 0:
            opposite_stage(1)
            x_stage(0)
            pass_on(halo_x, wx, relay_x)
    x_stage(1)


    def y_copy(d):
        return pltpu.make_async_remote_copy(
            src_ref=ys.at[d], dst_ref=yr.at[d], send_sem=ys_send.at[d],
            recv_sem=ys_recv.at[d], device_id=y_devs[d], device_id_type=MESH)

    def add_x(k, _):
        s2[k] = quarter(k, x) + xr[0, k].astype(F32) + xr[1, k].astype(F32)
        return 0

    def y_stage():
        for j in range(2):
            for d in range(2):
                x_copy(d, j).wait_recv()
        lax.fori_loop(0, K, add_x, 0)
        for d in range(3):
            ys[d] = s2[pl.ds(((y + d + 1) % 4) * 2, 2)].astype(BF16)
            y_copy(d).start()

    def while_forward(n):
        if n == 3:
            y_stage()

    convolve(halo_x, wx, rst_x, ((0, 1, 2), (), ()), while_forward)

    def z_copy(d):
        a, b = z_steps[d]
        src = s3.at[(zl + a) % 2, pl.ds(pl.multiple_of(((zh + b) % 2) * 24, 8), 24)]
        return pltpu.make_async_remote_copy(
            src_ref=src, dst_ref=zr.at[d], send_sem=zs_send.at[d],
            recv_sem=zs_recv.at[d], device_id=z_devs[d], device_id_type=MESH)

    def z_stage():
        for d in range(3):
            y_copy(d).wait_recv()
        s3[...] = s2[pl.ds(y * 2, 2)] + sum(yr[d].astype(F32) for d in range(3))
        for d in range(3):
            z_copy(d).start()

    def narrow(wide, result, to, sems):
        copies = []
        for third in range(3):
            for j in range(3 * third, 3 * third + 3):
                ten = pl.ds(j * 10 * rows, 10 * rows)
                block = jnp.concatenate([wide[n, ten] for n in range(tiles)], axis=1)
                result[pl.ds(j * 10, 10)] = block.astype(BF16).reshape(10, rows, C)
            piece = pl.ds(third * 30, 30)
            copies.append(
                pltpu.make_async_copy(result.at[piece], to.at[piece], sems.at[third]))
            copies[-1].start()
        return copies

    for j in range(2):
        if j == 0:
            for p in range(rows):
                for n in range(tiles):
                    flat[n, pl.ds(p, cols, stride=rows)] = (
                        own_c[p, 0:cols, n * 128:(n + 1) * 128].astype(F32))
        else:
            z_stage()
            stores = narrow(flat, gin_ref, gin_hbm, store_sem.at[0])
        acc = mix(j, weight)
        for i in range(per):
            for n in range(tiles):
                flat_out[n, pl.ds(j * per + i, cols, stride=rows)] = (
                    acc[i * 2 * B:i * 2 * B + cols, n * 128:(n + 1) * 128])
    stores += narrow(flat_out, out_ref, out_hbm, store_sem.at[1])

    for d in range(3):
        z_copy(d).wait_recv()
    total = s3[zl, pl.ds(pl.multiple_of(zh * 24, 8), 24)] + sum(zr[d] for d in range(3))
    scale = 1.0 / math.sqrt(rows * nlat * cols * nlon)
    gw_ref[...] = total * scale

    for copy in stores:
        copy.wait()
    for plan in (halo_c, halo_x):
        sent(plan, (0, 1, 2, 8, 9, 10, 11, 12, 13, 14, 15) + ((3, 4, 5, 6, 7) if plan is halo_x else ()))
    for j in range(2):
        core_copy(j).wait_send()
        for d in range(2):
            relay_copy(j, d).wait_send()
            x_copy(d, j).wait_send()
    for d in range(3):
        y_copy(d).wait_send()
        z_copy(d).wait_send()


def hand_over(out, gin, gw, out_to, gin_to, gw_to, out_v, gin_v, gw_v, sem_in, sem_out):
    parts = 3
    n = out.shape[0] // parts
    moves = []
    for i in range(parts):
        piece = pl.ds(i * n, n)
        moves.append((out.at[piece], out_v.at[piece], out_to.at[piece]))
        moves.append((gin.at[piece], gin_v.at[piece], gin_to.at[piece]))
    moves.append((gw, gw_v, gw_to))
    arriving = [
        pltpu.make_async_copy(a, b, sem_in.at[i]) for i, (a, b, _) in enumerate(moves)]
    leaving = [
        pltpu.make_async_copy(b, c, sem_out.at[i]) for i, (_, b, c) in enumerate(moves)]
    for copy in arriving:
        copy.start()
    for first, second in zip(arriving, leaving):
        first.wait()
        second.start()
    for copy in leaving:
        copy.wait()


def shards(inputs, basis, spans, weight, cotangent):
    rows, cols, C = inputs.shape
    K = weight.shape[0] // C
    nrows = basis.shape[0]
    by_lon = (1, 0, 2)
    ext = rows + 2 * RR
    vmem = pl.BlockSpec(memory_space=pltpu.VMEM)
    anywhere = pl.BlockSpec(memory_space=pl.ANY)
    own_cols = 2 * B
    dma = pltpu.SemaphoreType.DMA
    half = C // 2
    scratch = [
        pltpu.VMEM((cols, rows, C), BF16),
        pltpu.VMEM((cols, rows, C), BF16),
        pltpu.VMEM((ext, W, 2 * C), BF16),
        pltpu.VMEM((ext, W, 2 * C), BF16),
        pltpu.VMEM((rows, own_cols, C), BF16),
        pltpu.VMEM((rows, own_cols, C), BF16),
        pltpu.VMEM((rows, B, C), BF16),
        pltpu.VMEM((rows, B, C), BF16),
        pltpu.VMEM((ext, B, C), BF16),
        pltpu.VMEM((ext, B, C), BF16),
        pltpu.VMEM((2, RR, B, C), BF16),
        pltpu.VMEM((2, RR, B, C), BF16),
        pltpu.VMEM((C // 128, cols * rows, 128), F32),
        pltpu.VMEM((C // 128, cols * rows, 128), F32),
        pltpu.VMEM((rows, K * B, BAND), BF16),
        pltpu.VMEM((rows * own_cols, K * C), BF16),
        pltpu.VMEM((K * C, C), BF16),
        pltpu.VMEM((K * C, C), BF16),
        pltpu.VMEM((C, rows * own_cols), BF16),
        pltpu.VMEM((REACH, TAPS, K, nrows), BF16),
        pltpu.VMEM((REACH * TAPS * K, nrows), F32),
        pltpu.VMEM((BAND, nrows), F32),
        pltpu.VMEM((nrows + 16, BAND), F32),
        pltpu.VMEM((BAND // 128, 2 * rows * K, 128), F32),
        pltpu.VMEM((ext, K, BAND), F32),
        pltpu.VMEM((ext, K, BAND), F32),
        pltpu.VMEM((2, C, C), F32),
        pltpu.VMEM((K, half, C), F32),
        pltpu.VMEM((K, half, C), BF16),
        pltpu.VMEM((K, half, C), BF16),
        pltpu.VMEM((2, K // 2, half // 4, C), BF16),
        pltpu.VMEM((2, K // 2, half // 4, C), BF16),
        pltpu.VMEM((2, K, half // 4, C), BF16),
        pltpu.VMEM((2, K, half // 4, C), BF16),
        pltpu.VMEM((K, half // 4, C), F32),
        pltpu.VMEM((3, 2, half // 4, C), BF16),
        pltpu.VMEM((3, 2, half // 4, C), BF16),
        pltpu.VMEM((2, half // 4, C), F32),
        pltpu.VMEM((3, half // 8, C), F32),
        dma((4,)), dma((2, 3)),
        dma((2, 16)), dma((2, 12)),
        dma((2,)), dma((2,)),
        dma((2, 2)), dma((2, 2)),
        dma((2, 2)), dma((2, 2)),
        dma((3,)), dma((3,)),
        dma((3,)), dma((3,)),
    ]
    results = pl.pallas_call(
        kernel,
        out_shape=(
            jax.ShapeDtypeStruct((cols, rows, C), BF16),
            jax.ShapeDtypeStruct((cols, rows, C), BF16),
            jax.ShapeDtypeStruct((half // 8, C), F32),
        ),
        in_specs=[pl.BlockSpec(memory_space=pltpu.SMEM)] + [anywhere] * 4,
        out_specs=(anywhere, anywhere, vmem),
        scratch_shapes=scratch,
        compiler_params=pltpu.CompilerParams(
            collective_id=0, has_side_effects=True, vmem_limit_bytes=62 * 2**20),
    )(spans, cotangent.transpose(by_lon), inputs.transpose(by_lon),
      basis.transpose(2, 3, 1, 0), weight)
    output, grad_inputs, grad_weight = pl.pallas_call(
        hand_over,
        out_shape=[jax.ShapeDtypeStruct(r.shape, r.dtype) for r in results],
        in_specs=[anywhere] * 3,
        out_specs=[anywhere] * 3,
        scratch_shapes=[pltpu.VMEM(r.shape, r.dtype) for r in results] + [dma((7,)), dma((7,))],
    )(*results)
    return output.transpose(by_lon), grad_inputs.transpose(by_lon), grad_weight


def solution(mesh):
    in_specs = (P("lat", "lon", None), P(), P(), P(), P("lat", "lon", None))
    out_specs = (P("lat", "lon", None), P("lat", "lon", None), P(("lon", "lat"), None))
    return jax.shard_map(shards, mesh=mesh, in_specs=in_specs, out_specs=out_specs, check_vma=False)
```
